128 devices in a mesh: dp: 4 (over x), seq: 32 (over z, y, core).
Axes of the slice: x: 4, y: 4, z: 4, core: 2. Of those that a mesh axis runs over, the one named last changes fastest.
Arguments:
- hidden: bfloat16 [4, 12288, 2048], P('dp', 'seq')
- grad_out: bfloat16 [4, 12288, 2048], P('dp', 'seq'), may hold values from -6 to 6
- nbr_owner: int32 [4, 192, 2], P('dp', 'seq'), may hold values from 0 to 31, as said below
- send_slots: int32 [4, 32, 32, 1], P('dp', 'seq'), may hold values from 0 to 11
- encodings: bfloat16 [4, 384, 128, 896], P('dp', 'seq'), may hold values from -6 to 6
- weight_query: bfloat16 [2048, 1024], replicated, may hold values from -0.125 to 0.125
- weight_key: bfloat16 [896, 1024], replicated, may hold values from -0.1875 to 0.1875
- weight_value: bfloat16 [896, 1024], replicated, may hold values from -0.1875 to 0.1875
- weight_out: bfloat16 [1024, 2048], replicated, may hold values from -0.1875 to 0.1875
Outputs:
- mixed: bfloat16 [4, 12288, 2048], P('dp', 'seq')
- grad_hidden: bfloat16 [4, 12288, 2048], P('dp', 'seq')
- grad_encodings: bfloat16 [4, 384, 128, 896], P('dp', 'seq')
- grad_query: float32 [2048, 1024], P(('dp', 'seq'))
- grad_key: float32 [896, 1024], P(('dp', 'seq'))
- grad_value: float32 [896, 1024], P(('dp', 'seq'))
- grad_proj: float32 [1024, 2048], P(('dp', 'seq'))
The draws below stay inside these ranges and needn't reach their ends.
Inputs may be any that keep to these rules, and one draw needn't show every extreme that they name: `nbr_owner`: the 12 requests of one device name any one owner at most 1 times; in each sequence some owner is named exactly 1 times by every device.
All inputs are finite; a program needn't handle non-finite values.
Results may differ from the reference program's by a relative error of at most 0.017.
The reference program's roundings to bfloat16 on the way count: a program that leaves them out, or rounds other values in their place, can miss the bound.
Values may be sent and summed in bfloat16 or wider, within the bound.
No kernel may reach another device: no remote copies, remote signals or barrier semaphores. Data moves between devices by JAX's collectives and lax.ppermute only.
A program may use at most 192 MiB of HBM per device.

```python
import jax
import jax.numpy as jnp
from jax import lax

D = 2048
HEADS = 8
ENC = 896
GROUP = 64
RLEN = 128
NBR = 2
HD = 1024
SEQS = 4
OWNERS = 32
SEQ_LEN = 12288
GROUPS = 192
REQ_DEV = 12
CAP = 1
SLOTS = 12
ENCODINGS = 384
N_SEQ = 32


def draw_hidden(key, part):
    key = jax.random.fold_in(key, 11)
    first_key = jax.random.fold_in(key, 0)
    values = jax.random.normal(first_key, (SEQS, SEQ_LEN, D), jnp.float32)
    return jnp.clip(values, -30.0, 30.0).astype(jnp.bfloat16)


def draw_nbr_owner(key, part):
    key = jax.random.fold_in(key, 23)
    hot_key, rest_key = jax.random.split(key)
    hot_owner = jax.random.randint(hot_key, (SEQS,), 0, OWNERS).astype(jnp.int32)
    candidates = jnp.repeat(jnp.arange(OWNERS, dtype=jnp.int32), CAP)

    def one_device(flat_id):
        device_key = jax.random.fold_in(rest_key, flat_id)
        order_key, mix_key = jax.random.split(device_key)
        hot_one = hot_owner[flat_id // OWNERS]
        ranking = jax.random.permutation(order_key, OWNERS * CAP).astype(jnp.int32)
        ranking = jnp.where(candidates == hot_one, ranking - OWNERS * CAP, ranking)
        chosen = candidates[jnp.argsort(ranking, stable=True)[:REQ_DEV]]
        return chosen[jax.random.permutation(mix_key, REQ_DEV)]
    table = jax.vmap(one_device)(jnp.arange(SEQS * OWNERS, dtype=jnp.int32))
    return table.reshape(SEQS, GROUPS, NBR).astype(jnp.int32)


def set_ends(array, own_key, least, top_value):
    dims = array.shape
    spot = [jax.random.randint(jax.random.fold_in(own_key, axis), (), 0, dims[axis]) for axis in range(len(dims))]
    array = array.at[tuple(spot)].set(least)
    longest = dims.index(max(dims))
    spot[longest] = (spot[longest] + 1) % dims[longest]
    return array.at[tuple(spot)].set(top_value)


def levels(stream_key, dims, cuts, least, largest):
    def one(position, shards_of):
        steps = jax.random.uniform(jax.random.fold_in(jax.random.fold_in(stream_key, 6), position), (shards_of,), jnp.float32, least / len(cuts), largest / len(cuts))
        return jnp.repeat(jnp.exp(steps), dims[position] // shards_of).reshape((-1,) + (1,) * (len(dims) - position - 1))

    factor_of = one(*cuts[0])
    for cut in cuts[1:]:
        factor_of = factor_of * one(*cut)
    return factor_of


def noise(stream_key, extent, deviation, reach, pieces=(), held_as=jnp.bfloat16):
    factor_of = levels(stream_key, extent, pieces, -0.22, 0.18) if pieces else 1.0
    array = jax.random.normal(stream_key, extent, jnp.float32) * deviation * factor_of
    return jnp.minimum(jnp.maximum(array, -reach), reach).astype(held_as)


def setup_inputs(seed: int = 0) -> dict:
    keys = jax.random.split(jax.random.key(seed), 10)
    return {
        "hidden": draw_hidden(jax.random.fold_in(keys[9], 71), 0),
        "grad_out": noise(keys[1], (SEQS, SEQ_LEN, D), 1.0, 6.0, ((0, 4), (1, 32))),
        "nbr_owner": draw_nbr_owner(jax.random.fold_in(keys[9], 71), 0),
        "send_slots": set_ends(jax.random.randint(keys[3], (SEQS, OWNERS, OWNERS, CAP), 0, SLOTS), jax.random.fold_in(keys[3], 1), 0, SLOTS - 1).astype(jnp.int32),
        "encodings": noise(keys[4], (SEQS, ENCODINGS, RLEN, ENC), 1.0, 6.0, ((0, 4), (1, 32))),
        "weight_query": noise(keys[5], (D, HD), D ** -0.5, 0.125),
        "weight_key": noise(keys[6], (ENC, HD), ENC ** -0.5, 0.1875),
        "weight_value": noise(keys[7], (ENC, HD), ENC ** -0.5, 0.1875),
        "weight_out": noise(keys[8], (HD, D), HD ** -0.5, 0.1875),
    }


def attend_block(query_rows, cot_rows, picked, weight_query, weight_key, weight_value, weight_out):
    tok_count, model_width = query_rows.shape
    group_count = tok_count // GROUP
    req_count = picked.shape[0]
    inner_width = weight_query.shape[1]
    head_size = inner_width // HEADS
    score_scale = head_size ** -0.5
    queries = jnp.dot(query_rows, weight_query, preferred_element_type=jnp.float32).astype(jnp.bfloat16)
    enc_rows = picked.reshape(req_count * RLEN, ENC)
    key_rows = jnp.dot(enc_rows, weight_key, preferred_element_type=jnp.float32).astype(jnp.bfloat16)
    value_rows = jnp.dot(enc_rows, weight_value, preferred_element_type=jnp.float32).astype(jnp.bfloat16)
    query_heads = queries.reshape(group_count, GROUP, HEADS, head_size).astype(jnp.float32)
    key_heads = key_rows.reshape(group_count, -1, HEADS, head_size).astype(jnp.float32)
    value_heads = value_rows.reshape(group_count, -1, HEADS, head_size).astype(jnp.float32)
    scores = jnp.einsum("cqhs,ckhs->chqk", query_heads, key_heads) * score_scale
    row_max = jnp.max(scores, axis=-1, keepdims=True)
    lifted = jnp.exp(scores - row_max)
    attn_probs = lifted / jnp.sum(lifted, axis=-1, keepdims=True)
    probs_b = attn_probs.astype(jnp.bfloat16)
    context = jnp.einsum("chqk,ckhs->cqhs", probs_b.astype(jnp.float32), value_heads)
    context = context.astype(jnp.bfloat16).reshape(tok_count, inner_width)
    mixed_rows = jnp.dot(context, weight_out, preferred_element_type=jnp.float32).astype(jnp.bfloat16)
    d_context = jnp.dot(cot_rows, weight_out.T, preferred_element_type=jnp.float32).astype(jnp.bfloat16)
    grad_proj = jnp.dot(context.T, cot_rows, preferred_element_type=jnp.float32)
    dctx_heads = d_context.reshape(group_count, GROUP, HEADS, head_size).astype(jnp.float32)
    d_probs = jnp.einsum("cqhs,ckhs->chqk", dctx_heads, value_heads)
    d_values = jnp.einsum("chqk,cqhs->ckhs", probs_b.astype(jnp.float32), dctx_heads).astype(jnp.bfloat16)
    inner_sum = jnp.sum(attn_probs * d_probs, axis=-1, keepdims=True)
    d_scores = (score_scale * attn_probs * (d_probs - inner_sum)).astype(jnp.bfloat16).astype(jnp.float32)
    d_queries = jnp.einsum("chqk,ckhs->cqhs", d_scores, key_heads).astype(jnp.bfloat16).reshape(tok_count, inner_width)
    d_keys = jnp.einsum("chqk,cqhs->ckhs", d_scores, query_heads).astype(jnp.bfloat16).reshape(-1, inner_width)
    d_values = d_values.reshape(-1, inner_width)
    grad_query = jnp.dot(query_rows.T, d_queries, preferred_element_type=jnp.float32)
    d_shifted = jnp.dot(d_queries, weight_query.T, preferred_element_type=jnp.float32).astype(jnp.bfloat16)
    grad_key = jnp.dot(enc_rows.T, d_keys, preferred_element_type=jnp.float32)
    grad_value = jnp.dot(enc_rows.T, d_values, preferred_element_type=jnp.float32)
    d_picked = jnp.dot(d_keys, weight_key.T, preferred_element_type=jnp.float32) + jnp.dot(d_values, weight_value.T, preferred_element_type=jnp.float32)
    d_picked = d_picked.astype(jnp.bfloat16).reshape(picked.shape)
    return mixed_rows, d_shifted, d_picked, grad_query, grad_key, grad_value, grad_proj


def reference(hidden, grad_out, nbr_owner, send_slots, encodings, weight_query, weight_key, weight_value, weight_out):
    rim_size = GROUP - 1
    mixed_all = []
    grad_hidden_all = []
    grad_enc_all = []
    grad_query = jnp.zeros((D, HD), jnp.float32)
    grad_key = jnp.zeros((ENC, HD), jnp.float32)
    grad_value = jnp.zeros((ENC, HD), jnp.float32)
    grad_proj = jnp.zeros((HD, D), jnp.float32)
    for seq_index in range(SEQS):
        zero_rows = jnp.zeros((rim_size, D), jnp.bfloat16)
        shifted = jnp.concatenate([hidden[seq_index, rim_size:], zero_rows], axis=0)
        shifted_grad = jnp.concatenate([grad_out[seq_index, rim_size:], zero_rows], axis=0)
        owners = nbr_owner[seq_index].reshape(N_SEQ, REQ_DEV).astype(jnp.int32)
        same_owner = owners[:, :, None] == owners[:, None, :]
        earlier = lax.broadcasted_iota(jnp.int32, (REQ_DEV, REQ_DEV), 1) < lax.broadcasted_iota(jnp.int32, (REQ_DEV, REQ_DEV), 0)
        rank_ids = jnp.sum(jnp.logical_and(same_owner, earlier[None]).astype(jnp.int32), axis=2)
        device_ids = jnp.broadcast_to(jnp.arange(N_SEQ, dtype=jnp.int32)[:, None], owners.shape)
        slot_ids = send_slots[seq_index][owners, device_ids, rank_ids].astype(jnp.int32)
        enc_ids = (owners * SLOTS + slot_ids).reshape(-1).astype(jnp.int32)
        picked = encodings[seq_index][enc_ids]
        mixed_rows, d_shifted, d_picked, part_q, part_k, part_v, part_o = attend_block(
            shifted, shifted_grad, picked, weight_query, weight_key, weight_value, weight_out)
        mixed_all.append(jnp.concatenate([zero_rows, mixed_rows[:SEQ_LEN - rim_size]], axis=0))
        grad_hidden_all.append(jnp.concatenate([zero_rows, d_shifted[:SEQ_LEN - rim_size]], axis=0))
        enc_total = jnp.zeros((ENCODINGS, RLEN, ENC), jnp.float32).at[enc_ids].add(d_picked.astype(jnp.float32))
        grad_enc_all.append(enc_total.astype(jnp.bfloat16))
        grad_query = grad_query + part_q
        grad_key = grad_key + part_k
        grad_value = grad_value + part_v
        grad_proj = grad_proj + part_o
    return (jnp.stack(mixed_all), jnp.stack(grad_hidden_all), jnp.stack(grad_enc_all),
            grad_query, grad_key, grad_value, grad_proj)
```

```python
import functools

import jax
import jax.numpy as jnp
from jax import lax
from jax.experimental import pallas as pl
from jax.experimental.pallas import tpu as pltpu
from jax.sharding import PartitionSpec as P

HEADS = 8
GROUP = 64
NBR = 2

F32 = jnp.float32
BF16 = jnp.bfloat16


def nn(a, b):
    return lax.dot_general(a, b, (((1,), (0,)), ((), ())), preferred_element_type=F32)


def nt(a, b):
    return lax.dot_general(a, b, (((1,), (1,)), ((), ())), preferred_element_type=F32)


def tn(a, b):
    return lax.dot_general(a, b, (((0,), (0,)), ((), ())), preferred_element_type=F32)


def passed_along(x, axis, by):
    count = lax.axis_size(axis)
    pairs = [(i, i + by) for i in range(count) if 0 <= i + by < count]
    return lax.ppermute(x, axis, pairs)


def swapped(x):
    count = lax.axis_size("seq")
    return lax.ppermute(x, "seq", [(i, i ^ 1) for i in range(count)])


def attend_kernel(
    pos,
    named,
    core,
    enc_a,
    enc_b,
    q_ref,
    dc_ref,
    wk,
    wv,
    wkt,
    wvt,
    ctx_ref,
    dq_ref,
    dq_mine,
    dq_other,
    dk_mine,
    dk_other,
    dv_mine,
    dv_other,
    rows_ref,
    back_ref,
    k_all,
    v_all,
    dk_all,
    dv_all,
    d_rows,
    blank,
    sent,
    blanked,
):
    rlen = enc_a.shape[1]
    inner = q_ref.shape[1]
    size = inner // HEADS
    half_heads = HEADS // 2
    scale = size**-0.5
    step = pl.program_id(0)
    last = pl.num_programs(0) - 1

    def blanking(act):
        for owner in range(back_ref.shape[0]):

            @pl.when(named[owner] == 0)
            def _():
                act(pltpu.make_async_copy(blank, back_ref.at[owner], blanked))

    @pl.when(step == 0)
    def _():
        blank[...] = jnp.zeros_like(blank)
        blanking(lambda copy: copy.start())

    rows_ref[0:rlen, :] = enc_a[0]
    rows_ref[rlen : 2 * rlen, :] = enc_b[0]
    rows = rows_ref[...]
    k_all[...] = nn(rows, wk[...]).astype(BF16)
    v_all[...] = nn(rows, wv[...]).astype(BF16)
    units = []
    for side, halves in enumerate(
        ((dq_mine, dk_mine, dv_mine), (dq_other, dk_other, dv_other))
    ):
        half = core[0] if side == 0 else 1 - core[0]
        for h in range(half_heads):
            cols = pl.ds(pl.multiple_of(half * (inner // 2) + h * size, size), size)
            units.append((cols, slice(h * size, (h + 1) * size)) + halves)
    scores = [nt(q_ref[:, u[0]], k_all[:, u[0]]) * scale for u in units]
    d_probs = [nt(dc_ref[:, u[0]], v_all[:, u[0]]) for u in units]
    lifted = [jnp.exp(s - jnp.max(s, axis=-1, keepdims=True)) for s in scores]
    probs = [x * (1.0 / jnp.sum(x, axis=-1, keepdims=True)) for x in lifted]
    probs_b = [p.astype(BF16) for p in probs]
    for (cols, here, _, _, dv_half), p in zip(units, probs_b):
        ctx_ref[:, cols] = nn(p, v_all[:, cols]).astype(BF16)
    for (cols, here, _, _, dv_half), p in zip(units, probs_b):
        dv = tn(p, dc_ref[:, cols]).astype(BF16)
        dv_all[:, cols] = dv
        dv_half[:, here] = dv
    d_scores = [
        (scale * p * (d - jnp.sum(p * d, axis=-1, keepdims=True))).astype(BF16)
        for p, d in zip(probs, d_probs)
    ]
    for (cols, here, dq_half, _, _), d in zip(units, d_scores):
        dq = nn(d, k_all[:, cols]).astype(BF16)
        dq_ref[:, cols] = dq
        dq_half[:, here] = dq
    for (cols, here, _, dk_half, _), d in zip(units, d_scores):
        dk = tn(d, q_ref[:, cols]).astype(BF16)
        dk_all[:, cols] = dk
        dk_half[:, here] = dk

    def sending(at):
        return [
            pltpu.make_async_copy(d_rows.at[n], back_ref.at[pos[NBR * at + n]], sent.at[n])
            for n in range(NBR)
        ]

    @pl.when(step > 0)
    def _():
        for copy in sending(step - 1):
            copy.wait()

    for n in range(NBR):
        mine = slice(n * rlen, (n + 1) * rlen)
        total = nn(dk_all[mine, :], wkt[...]) + nn(dv_all[mine, :], wvt[...])
        d_rows[n] = total.astype(BF16)
    for copy in sending(step):
        copy.start()

    @pl.when(step == last)
    def _():
        for copy in sending(step):
            copy.wait()
        blanking(lambda copy: copy.wait())


def attend(pos, named, core, incoming, queries, d_context, wk, wv, wkt, wvt):
    owners, rlen, enc = incoming.shape
    toks, inner = queries.shape
    groups = toks // GROUP
    keys = NBR * rlen
    half = inner // 2

    def whole(x):
        return pl.BlockSpec(x.shape, lambda c, *_: (0, 0))

    def by_group(rows, cols):
        return pl.BlockSpec((rows, cols), lambda c, *_: (c, 0))

    grid_spec = pltpu.PrefetchScalarGridSpec(
        num_scalar_prefetch=3,
        grid=(groups,),
        in_specs=[
            pl.BlockSpec((1, rlen, enc), lambda c, pos, named, core: (pos[NBR * c], 0, 0)),
            pl.BlockSpec((1, rlen, enc), lambda c, pos, named, core: (pos[NBR * c + 1], 0, 0)),
            by_group(GROUP, inner),
            by_group(GROUP, inner),
            whole(wk),
            whole(wv),
            whole(wkt),
            whole(wvt),
        ],
        out_specs=[
            by_group(GROUP, inner),
            by_group(GROUP, inner),
            by_group(GROUP, half),
            by_group(GROUP, half),
            by_group(keys, half),
            by_group(keys, half),
            by_group(keys, half),
            by_group(keys, half),
            by_group(keys, enc),
            pl.BlockSpec(memory_space=pl.ANY),
        ],
        scratch_shapes=[pltpu.VMEM((keys, inner), BF16)] * 4
        + [
            pltpu.VMEM((NBR, rlen, enc), BF16),
            pltpu.VMEM((rlen, enc), BF16),
            pltpu.SemaphoreType.DMA((NBR,)),
            pltpu.SemaphoreType.DMA,
        ],
    )
    tok = jax.ShapeDtypeStruct((toks, inner), BF16)
    tok_half = jax.ShapeDtypeStruct((toks, half), BF16)
    key_half = jax.ShapeDtypeStruct((groups * keys, half), BF16)
    flops = 2 * groups * keys * enc * inner * 4 + 14 * toks * keys * inner
    return pl.pallas_call(
        attend_kernel,
        grid_spec=grid_spec,
        out_shape=[
            tok,
            tok,
            tok_half,
            tok_half,
            key_half,
            key_half,
            key_half,
            key_half,
            jax.ShapeDtypeStruct((groups * keys, enc), BF16),
            jax.ShapeDtypeStruct(incoming.shape, BF16),
        ],
        compiler_params=pltpu.CompilerParams(vmem_limit_bytes=36 * 1024 * 1024),
        cost_estimate=pl.CostEstimate(
            flops=flops, bytes_accessed=40_000_000, transcendentals=toks * keys * HEADS
        ),
        name="attend",
    )(pos, named, core, incoming, incoming, queries, d_context, wk, wv, wkt, wvt)


def fold_kernel(slot_ids, x_ref, out_ref, total):
    total[...] = jnp.zeros_like(total)
    for i in range(x_ref.shape[0]):
        total[slot_ids[i]] += x_ref[i].astype(F32)
    out_ref[...] = total[...].astype(BF16)


def fold(slot_ids, returned, slots):
    count, rlen, enc = returned.shape
    rows = 16
    return pl.pallas_call(
        fold_kernel,
        grid_spec=pltpu.PrefetchScalarGridSpec(
            num_scalar_prefetch=1,
            grid=(rlen // rows,),
            in_specs=[pl.BlockSpec((count, rows, enc), lambda i, s: (0, i, 0))],
            out_specs=pl.BlockSpec((slots, rows, enc), lambda i, s: (0, i, 0)),
            scratch_shapes=[pltpu.VMEM((slots, rows, enc), F32)],
        ),
        out_shape=jax.ShapeDtypeStruct((slots, rlen, enc), BF16),
        compiler_params=pltpu.CompilerParams(vmem_limit_bytes=24 * 1024 * 1024),
        cost_estimate=pl.CostEstimate(
            flops=count * rlen * enc,
            bytes_accessed=2 * (count + slots) * rlen * enc,
            transcendentals=0,
        ),
        name="fold",
    )(slot_ids, returned)


def partial_kernel(here, a_own, b_own, a_peer, b_peer, out_ref, top_ref, total):
    ring, rows, lanes = out_ref.shape
    chunk = total.shape[0] // ring
    total[...] = tn(a_own[...], b_own[...]) + tn(a_peer[...], b_peer[...])
    top = jnp.zeros((8, lanes), F32)
    for by in range(ring):
        at = pl.multiple_of(lax.rem(here[0] + by, ring) * chunk, 8)
        for n in range(total.shape[1] // lanes):
            piece = total[pl.ds(at, chunk), n * lanes : (n + 1) * lanes]
            out_ref[by, n * chunk : (n + 1) * chunk, :] = piece
            top = jnp.maximum(top, jnp.max(jnp.abs(piece).reshape(-1, 8, lanes), axis=0))
    top_ref[...] = top


def partial(here, lanes, a_own, b_own, a_peer, b_peer):
    ring = lax.axis_size("dp")
    toks, rows = a_own.shape
    cols = b_own.shape[1]
    out, top = pl.pallas_call(
        partial_kernel,
        grid_spec=pltpu.PrefetchScalarGridSpec(
            num_scalar_prefetch=1,
            grid=(1,),
            in_specs=[
                pl.BlockSpec(x.shape, lambda i, h: (0, 0)) for x in (a_own, b_own, a_peer, b_peer)
            ],
            out_specs=[
                pl.BlockSpec(
                    (ring, rows * cols // (lanes * ring), lanes), lambda i, h: (0, 0, 0)
                ),
                pl.BlockSpec((8, lanes), lambda i, h: (0, 0)),
            ],
            scratch_shapes=[pltpu.VMEM((rows, cols), F32)],
        ),
        out_shape=[
            jax.ShapeDtypeStruct((ring, rows * cols // (lanes * ring), lanes), F32),
            jax.ShapeDtypeStruct((8, lanes), F32),
        ],
        compiler_params=pltpu.CompilerParams(vmem_limit_bytes=40 * 1024 * 1024),
        cost_estimate=pl.CostEstimate(
            flops=4 * toks * rows * cols,
            bytes_accessed=4 * toks * (rows + cols) + 4 * rows * cols,
            transcendentals=0,
        ),
        name="partial",
    )(here, a_own, b_own, a_peer, b_peer)
    power = jnp.clip(jnp.floor(jnp.log2(jnp.max(top))), -100.0, 127.0)
    return out, power


def to_half(x, power):
    return (x * jnp.exp2(14.0 - power)).astype(jnp.float16)


def from_half(x, power):
    return x.astype(F32) * jnp.exp2(power - 14.0)


def packed(x, power):
    head = jnp.broadcast_to(power.astype(jnp.float16), (16, x.shape[1]))
    return jnp.concatenate([to_half(x, power), head], axis=0)


def unpacked(block):
    size = block.shape[0] - 16
    power = block[size, 0].astype(F32)
    return from_half(block[:size], power), power


def above(*powers):
    top = functools.reduce(jnp.maximum, powers)
    return jnp.clip(top + float(len(powers) - 1), -100.0, 127.0)


def summed_over_chips(a, a_power, b, b_power):
    ring = lax.axis_size("dp")
    assert ring == 4
    ahead = [(i, (i + 1) % ring) for i in range(ring)]
    behind = [(i, (i - 1) % ring) for i in range(ring)]
    far_a = lax.ppermute(packed(a[2], a_power), "dp", ahead)
    far_b = lax.ppermute(packed(b[2], b_power), "dp", behind)
    near_a = lax.ppermute(packed(a[3], a_power), "dp", behind)
    near_b = lax.ppermute(packed(b[1], b_power), "dp", ahead)

    def added(block, own, power):
        piece, theirs = unpacked(block)
        return packed(own + piece, above(power, theirs))

    two_a = lax.ppermute(added(far_a, a[1], a_power), "dp", ahead)
    two_b = lax.ppermute(added(far_b, b[3], b_power), "dp", behind)

    def closed(own, power, near, two):
        near, near_power = unpacked(near)
        two, two_power = unpacked(two)
        return own + near + two, above(power, near_power, two_power)

    return closed(a[0], a_power, near_a, two_a), closed(b[0], b_power, near_b, two_b)


def summed_over_seq(q, o, k, v):
    count = lax.axis_size("seq")
    lanes = q[0].shape[1]
    powers = [x[1] for x in (q, o, k, v)]
    q, o, k, v = (to_half(*x) for x in (q, o, k, v))
    both = o.shape[0] // (2 * count)
    q = q.reshape(count, -1, lanes)
    o = jnp.moveaxis(o.reshape(2, count, both, lanes), 0, 1).reshape(count, 2 * both, lanes)
    head = jnp.concatenate(
        [jnp.full((count, 2, lanes // 4), p.astype(jnp.float16)) for p in powers], axis=2
    )
    kv = jnp.concatenate([k.reshape(count, -1, lanes), v.reshape(count, -1, lanes), head], axis=1)
    q, o, kv = lax.optimization_barrier((q, o, kv))
    sent = jnp.concatenate([q, o, kv], axis=1)
    got = lax.all_to_all(sent, "seq", split_axis=0, concat_axis=0, tiled=True)
    outs, at, tail = [], 0, sent.shape[1] - 2
    for i, size in enumerate((q.shape[1], o.shape[1], k.shape[0] // count, v.shape[0] // count)):
        power = got[:, tail, i * (lanes // 4)].astype(F32).reshape(count // 2, 2, 1, 1)
        block = got[:, at : at + size].reshape(count // 2, 2, size, lanes)
        outs.append(jnp.sum(from_half(block, power), axis=0))
        at += size
    q, o, k, v = outs
    o = jnp.transpose(o.reshape(2, 2, both, lanes), (2, 0, 1, 3)).reshape(both, 4 * lanes)
    q, k, v = (jnp.moveaxis(x, 0, 1).reshape(x.shape[1], 2 * lanes) for x in (q, k, v))
    return q, o, k, v


def local(
    hidden,
    grad_out,
    nbr_owner,
    send_slots,
    encodings,
    weight_query,
    weight_key,
    weight_value,
    weight_out,
):
    rim = GROUP - 1
    tok_rows = hidden[0]
    cot_rows = grad_out[0]
    toks, width = tok_rows.shape
    own = encodings[0]
    slots, rlen, enc = own.shape
    count = lax.axis_size("seq")
    core = lax.rem(lax.axis_index("seq"), 2)
    first = core == 0

    head_rows, head_cot = passed_along((tok_rows[:rim], cot_rows[:rim]), "seq", -1)

    slot_ids = send_slots[0, 0].reshape(-1)
    outgoing = own.at[slot_ids].get(mode="promise_in_bounds")
    outgoing, head_rows, head_cot = lax.optimization_barrier((outgoing, head_rows, head_cot))
    incoming = lax.all_to_all(outgoing, "seq", split_axis=0, concat_axis=0, tiled=True)
    pos = nbr_owner[0].reshape(-1)

    query_rows = jnp.concatenate([tok_rows[rim:], head_rows], axis=0)
    grad_rows = jnp.concatenate([cot_rows[rim:], head_cot], axis=0)
    queries = nn(query_rows, weight_query).astype(BF16)
    d_context = nt(grad_rows, weight_out).astype(BF16)
    left, right = grad_rows[:, : width // 2], grad_rows[:, width // 2 :]
    grad_mine = jnp.where(first, left, right)
    query_peer, grad_peer = swapped((query_rows, jnp.where(first, right, left)))
    owner_ids = lax.broadcasted_iota(jnp.int32, (count, pos.shape[0]), 0)
    named = jnp.sum((owner_ids == pos[None, :]).astype(jnp.int32), axis=1)

    (
        context,
        d_queries,
        dq_mine,
        dq_other,
        dk_mine,
        dk_other,
        dv_mine,
        dv_other,
        rows,
        send_back,
    ) = attend(
        pos,
        named,
        core.reshape(1),
        incoming,
        queries,
        d_context,
        weight_key,
        weight_value,
        weight_key.T,
        weight_value.T,
    )
    returned = lax.all_to_all(send_back, "seq", split_axis=0, concat_axis=0, tiled=True)

    mixed_rows = nn(context, weight_out).astype(BF16)
    d_shifted = nt(d_queries, weight_query).astype(BF16)
    tail_mixed, tail_grad = passed_along(
        (mixed_rows[toks - rim :], d_shifted[toks - rim :]), "seq", 1
    )

    here = lax.axis_index("dp").reshape(1)
    half = dq_mine.shape[1]
    dq_peer, context_peer = swapped((dq_other, context))
    dk_peer, dv_peer, rows_peer = swapped((dk_other, dv_other, rows))
    part_q = partial(here, half, query_rows, dq_mine, query_peer, dq_peer)
    part_o = partial(here, half, context, grad_mine, context_peer, grad_peer)
    sum_q, sum_o = summed_over_chips(*part_q, *part_o)
    part_k = partial(here, half, rows, dk_mine, rows_peer, dk_peer)
    part_v = partial(here, half, rows, dv_mine, rows_peer, dv_peer)
    sum_k, sum_v = summed_over_chips(*part_k, *part_v)
    returned, sum_q, sum_o, sum_k, sum_v, tail_mixed, tail_grad = lax.optimization_barrier(
        (returned, sum_q, sum_o, sum_k, sum_v, tail_mixed, tail_grad)
    )
    share_q, share_o, share_k, share_v = summed_over_seq(sum_q, sum_o, sum_k, sum_v)
    mixed = jnp.concatenate([tail_mixed, mixed_rows[: toks - rim]], axis=0)[None]
    grad_hidden = jnp.concatenate([tail_grad, d_shifted[: toks - rim]], axis=0)[None]
    grad_own = fold(slot_ids, returned, slots)[None]
    return (mixed, grad_hidden, grad_own, share_q, share_k, share_v, share_o)


def solution(mesh):
    return jax.shard_map(
        local,
        mesh=mesh,
        in_specs=(
            P("dp", "seq", None),
            P("dp", "seq", None),
            P("dp", "seq", None),
            P("dp", "seq", None, None),
            P("dp", "seq", None, None),
            P(),
            P(),
            P(),
            P(),
        ),
        out_specs=(
            P("dp", "seq", None),
            P("dp", "seq", None),
            P("dp", "seq", None, None),
            P(("dp", "seq"), None),
            P(("dp", "seq"), None),
            P(("dp", "seq"), None),
            P(("dp", "seq"), None),
        ),
        check_vma=False,
    )
```

```python
import functools

import jax
import jax.numpy as jnp
from jax import lax
from jax.experimental import pallas as pl
from jax.experimental.pallas import tpu as pltpu
from jax.sharding import PartitionSpec as P

HEADS = 8
GROUP = 64
NBR = 2

F32 = jnp.float32
BF16 = jnp.bfloat16
HALF = jnp.float16
VMEM = 56 * 1024 * 1024


def nn(a, b):
    return lax.dot_general(a, b, (((1,), (0,)), ((), ())), preferred_element_type=F32)


def nt(a, b):
    return lax.dot_general(a, b, (((1,), (1,)), ((), ())), preferred_element_type=F32)


def tn(a, b):
    return lax.dot_general(a, b, (((0,), (0,)), ((), ())), preferred_element_type=F32)


def passed_along(x, axis, by):
    count = lax.axis_size(axis)
    pairs = [(i, i + by) for i in range(count) if 0 <= i + by < count]
    return lax.ppermute(x, axis, pairs)


def swapped(x):
    count = lax.axis_size("seq")
    return lax.ppermute(x, "seq", [(i, i ^ 1) for i in range(count)])


def attend_kernel(
    pos,
    named,
    core,
    enc_a,
    enc_b,
    q_ref,
    dc_ref,
    wk,
    wv,
    wkt,
    wvt,
    ctx_ref,
    dq_ref,
    dq_mine,
    dq_other,
    dk_mine,
    dk_other,
    dv_mine,
    dv_other,
    rows_ref,
    back_ref,
    k_all,
    v_all,
    dk_all,
    dv_all,
    d_rows,
    blank,
    sent,
    blanked,
):
    rlen = enc_a.shape[1]
    inner = q_ref.shape[1]
    size = inner // HEADS
    half_heads = HEADS // 2
    scale = size**-0.5
    step = pl.program_id(0)
    last = pl.num_programs(0) - 1

    def blanking(act):
        for owner in range(back_ref.shape[0]):

            @pl.when(named[owner] == 0)
            def _():
                act(pltpu.make_async_copy(blank, back_ref.at[owner], blanked))

    @pl.when(step == 0)
    def _():
        blank[...] = jnp.zeros_like(blank)
        blanking(lambda copy: copy.start())

    rows_ref[0:rlen, :] = enc_a[0]
    rows_ref[rlen : 2 * rlen, :] = enc_b[0]
    rows = rows_ref[...]
    k_all[...] = nn(rows, wk[...]).astype(BF16)
    v_all[...] = nn(rows, wv[...]).astype(BF16)
    units = []
    for side, halves in enumerate(
        ((dq_mine, dk_mine, dv_mine), (dq_other, dk_other, dv_other))
    ):
        half = core[0] if side == 0 else 1 - core[0]
        for h in range(half_heads):
            cols = pl.ds(pl.multiple_of(half * (inner // 2) + h * size, size), size)
            units.append((cols, slice(h * size, (h + 1) * size)) + halves)
    scores = [nt(q_ref[:, u[0]], k_all[:, u[0]]) * scale for u in units]
    d_probs = [nt(dc_ref[:, u[0]], v_all[:, u[0]]) for u in units]
    lifted = [jnp.exp(s - jnp.max(s, axis=-1, keepdims=True)) for s in scores]
    probs = [x * (1.0 / jnp.sum(x, axis=-1, keepdims=True)) for x in lifted]
    probs_b = [p.astype(BF16) for p in probs]
    for (cols, here, _, _, dv_half), p in zip(units, probs_b):
        ctx_ref[:, cols] = nn(p, v_all[:, cols]).astype(BF16)
    for (cols, here, _, _, dv_half), p in zip(units, probs_b):
        dv = tn(p, dc_ref[:, cols]).astype(BF16)
        dv_all[:, cols] = dv
        dv_half[:, here] = dv
    d_scores = [
        (scale * p * (d - jnp.sum(p * d, axis=-1, keepdims=True))).astype(BF16)
        for p, d in zip(probs, d_probs)
    ]
    for (cols, here, dq_half, _, _), d in zip(units, d_scores):
        dq = nn(d, k_all[:, cols]).astype(BF16)
        dq_ref[:, cols] = dq
        dq_half[:, here] = dq
    for (cols, here, _, dk_half, _), d in zip(units, d_scores):
        dk = tn(d, q_ref[:, cols]).astype(BF16)
        dk_all[:, cols] = dk
        dk_half[:, here] = dk

    def sending(at):
        return [
            pltpu.make_async_copy(d_rows.at[n], back_ref.at[pos[NBR * at + n]], sent.at[n])
            for n in range(NBR)
        ]

    @pl.when(step > 0)
    def _():
        for copy in sending(step - 1):
            copy.wait()

    for n in range(NBR):
        mine = slice(n * rlen, (n + 1) * rlen)
        total = nn(dk_all[mine, :], wkt[...]) + nn(dv_all[mine, :], wvt[...])
        d_rows[n] = total.astype(BF16)
    for copy in sending(step):
        copy.start()

    @pl.when(step == last)
    def _():
        for copy in sending(step):
            copy.wait()
        blanking(lambda copy: copy.wait())


def attend(pos, named, core, incoming, queries, d_context, wk, wv, wkt, wvt):
    owners, rlen, enc = incoming.shape
    toks, inner = queries.shape
    groups = toks // GROUP
    keys = NBR * rlen
    half = inner // 2

    def whole(x):
        return pl.BlockSpec(x.shape, lambda c, *_: (0, 0))

    def by_group(rows, cols):
        return pl.BlockSpec((rows, cols), lambda c, *_: (c, 0))

    grid_spec = pltpu.PrefetchScalarGridSpec(
        num_scalar_prefetch=3,
        grid=(groups,),
        in_specs=[
            pl.BlockSpec((1, rlen, enc), lambda c, pos, named, core: (pos[NBR * c], 0, 0)),
            pl.BlockSpec((1, rlen, enc), lambda c, pos, named, core: (pos[NBR * c + 1], 0, 0)),
            by_group(GROUP, inner),
            by_group(GROUP, inner),
            whole(wk),
            whole(wv),
            whole(wkt),
            whole(wvt),
        ],
        out_specs=[
            by_group(GROUP, inner),
            by_group(GROUP, inner),
            by_group(GROUP, half),
            by_group(GROUP, half),
            by_group(keys, half),
            by_group(keys, half),
            by_group(keys, half),
            by_group(keys, half),
            by_group(keys, enc),
            pl.BlockSpec(memory_space=pl.ANY),
        ],
        scratch_shapes=[pltpu.VMEM((keys, inner), BF16)] * 4
        + [
            pltpu.VMEM((NBR, rlen, enc), BF16),
            pltpu.VMEM((rlen, enc), BF16),
            pltpu.SemaphoreType.DMA((NBR,)),
            pltpu.SemaphoreType.DMA,
        ],
    )
    tok = jax.ShapeDtypeStruct((toks, inner), BF16)
    tok_half = jax.ShapeDtypeStruct((toks, half), BF16)
    key_half = jax.ShapeDtypeStruct((groups * keys, half), BF16)
    flops = 2 * groups * keys * enc * inner * 4 + 14 * toks * keys * inner
    return pl.pallas_call(
        attend_kernel,
        grid_spec=grid_spec,
        out_shape=[
            tok,
            tok,
            tok_half,
            tok_half,
            key_half,
            key_half,
            key_half,
            key_half,
            jax.ShapeDtypeStruct((groups * keys, enc), BF16),
            jax.ShapeDtypeStruct(incoming.shape, BF16),
        ],
        compiler_params=pltpu.CompilerParams(vmem_limit_bytes=VMEM),
        cost_estimate=pl.CostEstimate(
            flops=flops, bytes_accessed=40_000_000, transcendentals=toks * keys * HEADS
        ),
        name="attend",
    )(pos, named, core, incoming, incoming, queries, d_context, wk, wv, wkt, wvt)


def fold_kernel(slot_ids, x_ref, out_ref, total):
    total[...] = jnp.zeros_like(total)
    for i in range(x_ref.shape[0]):
        total[slot_ids[i]] += x_ref[i].astype(F32)
    out_ref[...] = total[...].astype(BF16)


def fold(slot_ids, returned, slots):
    count, rlen, enc = returned.shape
    rows = 16
    return pl.pallas_call(
        fold_kernel,
        grid_spec=pltpu.PrefetchScalarGridSpec(
            num_scalar_prefetch=1,
            grid=(rlen // rows,),
            in_specs=[pl.BlockSpec((count, rows, enc), lambda i, s: (0, i, 0))],
            out_specs=pl.BlockSpec((slots, rows, enc), lambda i, s: (0, i, 0)),
            scratch_shapes=[pltpu.VMEM((slots, rows, enc), F32)],
        ),
        out_shape=jax.ShapeDtypeStruct((slots, rlen, enc), BF16),
        compiler_params=pltpu.CompilerParams(vmem_limit_bytes=24 * 1024 * 1024),
        cost_estimate=pl.CostEstimate(
            flops=count * rlen * enc,
            bytes_accessed=2 * (count + slots) * rlen * enc,
            transcendentals=0,
        ),
        name="fold",
    )(slot_ids, returned)


def partial_kernel(layout, parts, here, *refs):
    ring = 4
    count = len(layout)
    a_own, a_peer = refs[:2]
    b_refs = refs[2 : 2 + 2 * count]
    outs = refs[2 + 2 * count : 2 + 2 * count + 4 * len(parts)]
    power_ref = refs[2 + 2 * count + 4 * len(parts)]
    totals = refs[3 + 2 * count + 4 * len(parts) :]
    lanes = outs[0].shape[1]
    powers = []
    for i, total in enumerate(totals):
        total[...] = tn(a_own[...], b_refs[2 * i][...]) + tn(a_peer[...], b_refs[2 * i + 1][...])
        top = jnp.max(jnp.abs(total[...]).reshape(-1, 8, total.shape[1]), axis=0)
        top = jnp.full((8, 128), jnp.max(top))
        powers.append(jnp.clip(jnp.floor(jnp.log2(top)), -100.0, 127.0))
    for i in range(2):
        power = powers[min(i, count - 1)]
        head = power * jnp.exp2(power - 14.0)
        for n in range(lanes // 128):
            at = slice(n * 128, (n + 1) * 128)
            power_ref[8 * i : 8 * i + 8, at] = power
            for out in outs:
                size = out.shape[0] - 16
                out[size + 8 * i : size + 8 * i + 8, at] = head

    def fill(out, by, first, end):
        pieces = []
        for total, (slices, rows, _) in zip(totals, layout):
            chunk = total.shape[0] // ring
            at = pl.multiple_of(lax.rem(here[0] + by, ring) * chunk, 8)
            for n in range(slices):
                pieces.append((total[pl.ds(at, chunk), n * lanes : (n + 1) * lanes], rows))
        at = 0
        if len(pieces) == 1:
            piece, rows = pieces[0]
            out[0 : (end - first) * rows, :] = piece[first * rows : end * rows]
            return
        for dest in range(first, end):
            for piece, rows in pieces:
                out[at : at + rows, :] = piece[dest * rows : (dest + 1) * rows]
                at += rows
                fill_up = -rows % 8
                if fill_up:
                    out[at : at + fill_up, :] = jnp.zeros((fill_up, lanes), F32)
                at += fill_up

    for n, (first, end, near_by, wait_by) in enumerate(parts):
        for out, by in zip(outs[4 * n : 4 * n + 4], (2, near_by, wait_by, 0)):
            fill(out, by, first, end)


def partial(here, lanes, a_own, a_peer, pairs, parts):
    count = lax.axis_size("seq")
    ring = lax.axis_size("dp")
    assert ring == 4
    toks, rows = a_own.shape
    per = rows // (ring * count)
    layout = [(b.shape[1] // lanes, per, -per % 8) for b, _ in pairs]
    size = sum(n * (r + fill) for n, r, fill in layout)
    operands = [a_own, a_peer] + [b for pair in pairs for b in pair]

    def whole(shape):
        return pl.BlockSpec(shape, lambda i, h: (0, 0))

    shapes = []
    for first, end, _, _ in parts:
        shapes += [((end - first) * size + 16, lanes)] * 4
    shapes.append((16, lanes))
    cols = sum(b.shape[1] for b, _ in pairs)
    outs = pl.pallas_call(
        functools.partial(partial_kernel, layout, parts),
        grid_spec=pltpu.PrefetchScalarGridSpec(
            num_scalar_prefetch=1,
            grid=(1,),
            in_specs=[whole(x.shape) for x in operands],
            out_specs=[whole(shape) for shape in shapes],
            scratch_shapes=[pltpu.VMEM((rows, b.shape[1]), F32) for b, _ in pairs],
        ),
        out_shape=[jax.ShapeDtypeStruct(shape, F32) for shape in shapes],
        compiler_params=pltpu.CompilerParams(vmem_limit_bytes=40 * 1024 * 1024),
        cost_estimate=pl.CostEstimate(
            flops=8 * toks * rows * cols,
            bytes_accessed=4 * toks * (rows + cols) + 4 * rows * cols,
            transcendentals=0,
        ),
        name="partial",
    )(here, *operands)
    powers = (outs[-1][0:1], outs[-1][8:9])
    return [outs[4 * n : 4 * n + 4] for n in range(len(parts))], powers


def by_row(shape, first, second):
    rows = lax.broadcasted_iota(jnp.int32, shape, 0)
    return jnp.where(lax.rem(rows, 16) < 8, first, second)


def up(shape, powers):
    return by_row(shape, *(jnp.exp2(14.0 - p) for p in powers))


def down(shape, powers):
    return by_row(shape, *(jnp.exp2(p - 14.0) for p in powers))


def above(*powers):
    tops = [functools.reduce(jnp.maximum, p) for p in zip(*powers)]
    return [jnp.clip(t + float(len(powers) - 1), -100.0, 127.0) for t in tops]


def moved(x, way):
    return lax.ppermute(x, "dp", [(i, (i + way) % 4) for i in range(4)])


def heads(x):
    return x[-16:-15].astype(F32), x[-8:-7].astype(F32)


def ring_start(part, powers):
    far, near = part[:2]
    return [(x * up(x.shape, powers)).astype(HALF) for x in (far, near)]


def ring_middle(part, powers, far):
    shape = far.shape
    theirs = heads(far)
    tops = above(powers, theirs)
    both = (part[2] + far.astype(F32) * down(shape, theirs)) * up(shape, tops)
    is_head = lax.broadcasted_iota(jnp.int32, shape, 0) >= shape[0] - 16
    return jnp.where(is_head, by_row(shape, *tops), both).astype(HALF)


def ring_end(part, powers, near, two):
    shape = near.shape
    near_powers, two_powers = heads(near), heads(two)
    total = (
        part[3]
        + near.astype(F32) * down(shape, near_powers)
        + two.astype(F32) * down(shape, two_powers)
    )
    return total, above(powers, near_powers, two_powers)


def for_seq(q, o, kv_low, kv_high):
    count = lax.axis_size("seq")
    lanes = q[0].shape[1]
    quarter = lanes // 4
    tops = [jnp.maximum(a, b) for a, b in zip(kv_low[1], kv_high[1])]
    powers = (q[1][0], o[1][0], tops[0], tops[1])

    def halves(x, tops):
        x = x[0][: x[0].shape[0] - 16]
        return (x * up(x.shape, tops)).astype(HALF)

    def with_powers(x):
        rows = lax.broadcasted_iota(jnp.int32, x.shape, 0)
        lane = lax.broadcasted_iota(jnp.int32, (1, lanes), 1) // quarter
        mark = jnp.where(
            lane < 2,
            jnp.where(lane == 0, powers[0], powers[1]),
            jnp.where(lane == 2, powers[2], powers[3]),
        )
        return jnp.where(lax.rem(rows, 16) == 7, mark.astype(HALF), x)

    blocks = (
        halves(q, q[1]),
        halves(o, o[1]),
        with_powers(halves(kv_low, tops)),
        with_powers(halves(kv_high, tops)),
    )
    q, o, kv_low, kv_high = lax.optimization_barrier(blocks)
    kv = jnp.concatenate([kv_low, kv_high], axis=0)
    q, o, kv = (x.reshape(count, -1, lanes) for x in (q, o, kv))
    return jnp.concatenate([q, o, kv], axis=1), q.shape[1], o.shape[1]


def summed_over_seq(sent, n_q, n_o):
    quarter = sent.shape[2] // 4
    got = lax.all_to_all(sent, "seq", split_axis=0, concat_axis=0, tiled=True)
    mark = n_q + n_o + 7
    row = lax.broadcasted_iota(jnp.int32, (1,) + got.shape[1:], 1)

    def widened(block):
        scales = [
            jnp.exp2(block[:, mark : mark + 1, i * quarter : i * quarter + 1].astype(F32) - 14.0)
            for i in range(4)
        ]
        scale = jnp.where(
            row < n_q,
            scales[0],
            jnp.where(
                row < n_q + n_o,
                scales[1],
                jnp.where(row < n_q + n_o + 8, scales[2], scales[3]),
            ),
        )
        return block.astype(F32) * scale

    total = functools.reduce(
        jnp.add, [widened(got[i : i + 2]) for i in range(0, got.shape[0], 2)]
    )

    def joined(first, rows, slices=1):
        return jnp.concatenate(
            [
                total[c, first + n * rows : first + (n + 1) * rows]
                for c in range(2)
                for n in range(slices)
            ],
            axis=1,
        )

    return (
        joined(0, n_q),
        joined(n_q, n_o // 2, 2),
        joined(n_q + n_o, 7),
        joined(n_q + n_o + 8, 7),
    )


def local(
    hidden,
    grad_out,
    nbr_owner,
    send_slots,
    encodings,
    weight_query,
    weight_key,
    weight_value,
    weight_out,
):
    rim = GROUP - 1
    tok_rows = hidden[0]
    cot_rows = grad_out[0]
    toks, width = tok_rows.shape
    own = encodings[0]
    slots, rlen, enc = own.shape
    count = lax.axis_size("seq")
    core = lax.rem(lax.axis_index("seq"), 2)
    is_first = core == 0

    heads = jnp.concatenate([tok_rows[:rim], cot_rows[:rim]], axis=1)
    heads = passed_along(heads, "seq", -1)

    slot_ids = send_slots[0, 0].reshape(-1)
    outgoing = own.at[slot_ids].get(mode="promise_in_bounds")
    outgoing, heads = lax.optimization_barrier((outgoing, heads))
    incoming = lax.all_to_all(outgoing, "seq", split_axis=0, concat_axis=0, tiled=True)
    pos = nbr_owner[0].reshape(-1)

    query_rows = jnp.concatenate([tok_rows[rim:], heads[:, :width]], axis=0)
    grad_rows = jnp.concatenate([cot_rows[rim:], heads[:, width:]], axis=0)
    queries = nn(query_rows, weight_query).astype(BF16)
    d_context = nt(grad_rows, weight_out).astype(BF16)
    left, right = grad_rows[:, : width // 2], grad_rows[:, width // 2 :]
    grad_mine = jnp.where(is_first, left, right)
    query_peer, grad_peer = swapped((query_rows, jnp.where(is_first, right, left)))
    queries, d_context, grad_mine = lax.optimization_barrier((queries, d_context, grad_mine))
    owner_ids = lax.broadcasted_iota(jnp.int32, (count, pos.shape[0]), 0)
    named = jnp.sum((owner_ids == pos[None, :]).astype(jnp.int32), axis=1)

    (
        context,
        d_queries,
        dq_mine,
        dq_other,
        dk_mine,
        dk_other,
        dv_mine,
        dv_other,
        rows,
        send_back,
    ) = attend(
        pos,
        named,
        core.reshape(1),
        incoming,
        queries,
        d_context,
        weight_key,
        weight_value,
        weight_key.T,
        weight_value.T,
    )
    returned = lax.all_to_all(send_back, "seq", split_axis=0, concat_axis=0, tiled=True)

    tails = jnp.concatenate([context[toks - rim :], d_queries[toks - rim :]], axis=1)
    tails = passed_along(tails, "seq", 1)

    here = lax.axis_index("dp").reshape(1)
    half = dq_mine.shape[1]
    dq_peer, context_peer = swapped((dq_other, context))
    dk_peer, dv_peer, rows_peer = swapped((dk_other, dv_other, rows))
    (part_q,), power_q = partial(
        here, half, query_rows, query_peer, [(dq_mine, dq_peer)], [(0, count, 3, 1)]
    )
    (part_o,), power_o = partial(
        here, half, context, context_peer, [(grad_mine, grad_peer)], [(0, count, 1, 3)]
    )
    ways = (1, -1)
    first = [ring_start(part_q, power_q), ring_start(part_o, power_o)]
    kv_inputs = (rows, rows_peer, dk_mine, dk_peer, dv_mine, dv_peer)
    first, kv_inputs = lax.optimization_barrier((first, kv_inputs))
    first = [[moved(far, w), moved(near, -w)] for (far, near), w in zip(first, ways)]
    (part_low, part_high), power_kv = partial(
        here,
        half,
        kv_inputs[0],
        kv_inputs[1],
        [kv_inputs[2:4], kv_inputs[4:6]],
        [(0, count // 2, 3, 1), (count // 2, count, 1, 3)],
    )
    second = [ring_start(part_low, power_kv), ring_start(part_high, power_kv)]
    first, second = lax.optimization_barrier((first, second))
    second = [[moved(far, w), moved(near, -w)] for (far, near), w in zip(second, ways)]
    two_q = ring_middle(part_q, power_q, first[0][0])
    two_o = ring_middle(part_o, power_o, first[1][0])
    two_q, two_o, second = lax.optimization_barrier((two_q, two_o, second))
    two_q, two_o = moved(two_q, 1), moved(two_o, -1)
    two_low = moved(ring_middle(part_low, power_kv, second[0][0]), 1)
    two_high = moved(ring_middle(part_high, power_kv, second[1][0]), -1)
    sum_q = ring_end(part_q, power_q, first[0][1], two_q)
    sum_o = ring_end(part_o, power_o, first[1][1], two_o)
    sum_low = ring_end(part_low, power_kv, second[0][1], two_low)
    sum_high = ring_end(part_high, power_kv, second[1][1], two_high)
    sent, n_q, n_o = for_seq(sum_q, sum_o, sum_low, sum_high)
    returned, sent, tails = lax.optimization_barrier((returned, sent, tails))
    share_q, share_o, share_k, share_v = summed_over_seq(sent, n_q, n_o)

    inner = context.shape[1]
    context = jnp.concatenate([tails[:, :inner], context[: toks - rim]], axis=0)
    d_queries = jnp.concatenate([tails[:, inner:], d_queries[: toks - rim]], axis=0)
    mixed = nn(context, weight_out).astype(BF16)[None]
    grad_hidden = nt(d_queries, weight_query).astype(BF16)[None]
    grad_own = fold(slot_ids, returned, slots)[None]
    return (mixed, grad_hidden, grad_own, share_q, share_k, share_v, share_o)


def solution(mesh):
    return jax.shard_map(
        local,
        mesh=mesh,
        in_specs=(
            P("dp", "seq", None),
            P("dp", "seq", None),
            P("dp", "seq", None),
            P("dp", "seq", None, None),
            P("dp", "seq", None, None),
            P(),
            P(),
            P(),
            P(),
        ),
        out_specs=(
            P("dp", "seq", None),
            P("dp", "seq", None),
            P("dp", "seq", None, None),
            P(("dp", "seq"), None),
            P(("dp", "seq"), None),
            P(("dp", "seq"), None),
            P(("dp", "seq"), None),
        ),
        check_vma=False,
    )
```

```python
import functools

import jax
import jax.numpy as jnp
from jax import lax
from jax.experimental import pallas as pl
from jax.experimental.pallas import tpu as pltpu
from jax.sharding import PartitionSpec as P

HEADS = 8
GROUP = 64
NBR = 2

F32 = jnp.float32
BF16 = jnp.bfloat16
HALF = jnp.float16
VMEM = 56 * 1024 * 1024


def nn(a, b):
    return lax.dot_general(a, b, (((1,), (0,)), ((), ())), preferred_element_type=F32)


def nt(a, b):
    return lax.dot_general(a, b, (((1,), (1,)), ((), ())), preferred_element_type=F32)


def tn(a, b):
    return lax.dot_general(a, b, (((0,), (0,)), ((), ())), preferred_element_type=F32)


def passed_along(x, axis, by):
    count = lax.axis_size(axis)
    pairs = [(i, i + by) for i in range(count) if 0 <= i + by < count]
    return lax.ppermute(x, axis, pairs)


def swapped(x):
    count = lax.axis_size("seq")
    return lax.ppermute(x, "seq", [(i, i ^ 1) for i in range(count)])


def attend_kernel(
    pos,
    named,
    core,
    enc_a,
    enc_b,
    q_ref,
    dc_ref,
    wk,
    wv,
    wkt,
    wvt,
    ctx_ref,
    dq_ref,
    dq_mine,
    dq_other,
    dk_mine,
    dk_other,
    dv_mine,
    dv_other,
    rows_ref,
    tail_ref,
    back_ref,
    k_all,
    v_all,
    dk_all,
    dv_all,
    d_rows,
    blank,
    sent,
    blanked,
):
    rlen = enc_a.shape[1]
    inner = q_ref.shape[1]
    size = inner // HEADS
    half_heads = HEADS // 2
    scale = size**-0.5
    step = pl.program_id(0)
    last = pl.num_programs(0) - 1

    def blanking(act):
        for owner in range(back_ref.shape[0]):

            @pl.when(named[owner] == 0)
            def _():
                act(pltpu.make_async_copy(blank, back_ref.at[owner], blanked))

    @pl.when(step == 0)
    def _():
        blank[...] = jnp.zeros_like(blank)
        blanking(lambda copy: copy.start())

    rows_ref[0:rlen, :] = enc_a[0]
    rows_ref[rlen : 2 * rlen, :] = enc_b[0]
    rows = rows_ref[...]
    k_all[...] = nn(rows, wk[...]).astype(BF16)
    v_all[...] = nn(rows, wv[...]).astype(BF16)
    units = []
    for side, halves in enumerate(
        ((dq_mine, dk_mine, dv_mine), (dq_other, dk_other, dv_other))
    ):
        half = core[0] if side == 0 else 1 - core[0]
        for h in range(half_heads):
            cols = pl.ds(pl.multiple_of(half * (inner // 2) + h * size, size), size)
            units.append((cols, slice(h * size, (h + 1) * size)) + halves)
    scores = [nt(q_ref[:, u[0]], k_all[:, u[0]]) * scale for u in units]
    d_probs = [nt(dc_ref[:, u[0]], v_all[:, u[0]]) for u in units]
    lifted = [jnp.exp(s - jnp.max(s, axis=-1, keepdims=True)) for s in scores]
    probs = [x * (1.0 / jnp.sum(x, axis=-1, keepdims=True)) for x in lifted]
    probs_b = [p.astype(BF16) for p in probs]
    for (cols, here, _, _, dv_half), p in zip(units, probs_b):
        ctx_ref[:, cols] = nn(p, v_all[:, cols]).astype(BF16)
    for (cols, here, _, _, dv_half), p in zip(units, probs_b):
        dv = tn(p, dc_ref[:, cols]).astype(BF16)
        dv_all[:, cols] = dv
        dv_half[:, here] = dv
    d_scores = [
        (scale * p * (d - jnp.sum(p * d, axis=-1, keepdims=True))).astype(BF16)
        for p, d in zip(probs, d_probs)
    ]
    for (cols, here, dq_half, _, _), d in zip(units, d_scores):
        dq = nn(d, k_all[:, cols]).astype(BF16)
        dq_ref[:, cols] = dq
        dq_half[:, here] = dq
    for (cols, here, _, dk_half, _), d in zip(units, d_scores):
        dk = tn(d, q_ref[:, cols]).astype(BF16)
        dk_all[:, cols] = dk
        dk_half[:, here] = dk

    def sending(at):
        return [
            pltpu.make_async_copy(d_rows.at[n], back_ref.at[pos[NBR * at + n]], sent.at[n])
            for n in range(NBR)
        ]

    @pl.when(step > 0)
    def _():
        for copy in sending(step - 1):
            copy.wait()

    for n in range(NBR):
        mine = slice(n * rlen, (n + 1) * rlen)
        total = nn(dk_all[mine, :], wkt[...]) + nn(dv_all[mine, :], wvt[...])
        d_rows[n] = total.astype(BF16)
    for copy in sending(step):
        copy.start()

    @pl.when(step == last)
    def _():
        tail_ref[:, :inner] = ctx_ref[...]
        tail_ref[:, inner:] = dq_ref[...]
        for copy in sending(step):
            copy.wait()
        blanking(lambda copy: copy.wait())


def attend(pos, named, core, incoming, queries, d_context, wk, wv, wkt, wvt):
    owners, rlen, enc = incoming.shape
    toks, inner = queries.shape
    groups = toks // GROUP
    keys = NBR * rlen
    half = inner // 2

    def whole(x):
        return pl.BlockSpec(x.shape, lambda c, *_: (0, 0))

    def by_group(rows, cols):
        return pl.BlockSpec((rows, cols), lambda c, *_: (c, 0))

    grid_spec = pltpu.PrefetchScalarGridSpec(
        num_scalar_prefetch=3,
        grid=(groups,),
        in_specs=[
            pl.BlockSpec((1, rlen, enc), lambda c, pos, named, core: (pos[NBR * c], 0, 0)),
            pl.BlockSpec((1, rlen, enc), lambda c, pos, named, core: (pos[NBR * c + 1], 0, 0)),
            by_group(GROUP, inner),
            by_group(GROUP, inner),
            whole(wk),
            whole(wv),
            whole(wkt),
            whole(wvt),
        ],
        out_specs=[
            by_group(GROUP, inner),
            by_group(GROUP, inner),
            by_group(GROUP, half),
            by_group(GROUP, half),
            by_group(keys, half),
            by_group(keys, half),
            by_group(keys, half),
            by_group(keys, half),
            by_group(keys, enc),
            pl.BlockSpec((GROUP, 2 * inner), lambda c, *_: (0, 0)),
            pl.BlockSpec(memory_space=pl.ANY),
        ],
        scratch_shapes=[pltpu.VMEM((keys, inner), BF16)] * 4
        + [
            pltpu.VMEM((NBR, rlen, enc), BF16),
            pltpu.VMEM((rlen, enc), BF16),
            pltpu.SemaphoreType.DMA((NBR,)),
            pltpu.SemaphoreType.DMA,
        ],
    )
    tok = jax.ShapeDtypeStruct((toks, inner), BF16)
    tok_half = jax.ShapeDtypeStruct((toks, half), BF16)
    key_half = jax.ShapeDtypeStruct((groups * keys, half), BF16)
    flops = 2 * groups * keys * enc * inner * 4 + 14 * toks * keys * inner
    return pl.pallas_call(
        attend_kernel,
        grid_spec=grid_spec,
        out_shape=[
            tok,
            tok,
            tok_half,
            tok_half,
            key_half,
            key_half,
            key_half,
            key_half,
            jax.ShapeDtypeStruct((groups * keys, enc), BF16),
            jax.ShapeDtypeStruct((GROUP, 2 * inner), BF16),
            jax.ShapeDtypeStruct(incoming.shape, BF16),
        ],
        compiler_params=pltpu.CompilerParams(vmem_limit_bytes=VMEM),
        cost_estimate=pl.CostEstimate(
            flops=flops, bytes_accessed=40_000_000, transcendentals=toks * keys * HEADS
        ),
        name="attend",
    )(pos, named, core, incoming, incoming, queries, d_context, wk, wv, wkt, wvt)


def fold_kernel(slot_ids, x_ref, out_ref, total):
    total[...] = jnp.zeros_like(total)
    for i in range(x_ref.shape[0]):
        total[slot_ids[i]] += x_ref[i].astype(F32)
    out_ref[...] = total[...].astype(BF16)


def fold(slot_ids, returned, slots):
    count, rlen, enc = returned.shape
    rows = 16
    return pl.pallas_call(
        fold_kernel,
        grid_spec=pltpu.PrefetchScalarGridSpec(
            num_scalar_prefetch=1,
            grid=(rlen // rows,),
            in_specs=[pl.BlockSpec((count, rows, enc), lambda i, s: (0, i, 0))],
            out_specs=pl.BlockSpec((slots, rows, enc), lambda i, s: (0, i, 0)),
            scratch_shapes=[pltpu.VMEM((slots, rows, enc), F32)],
        ),
        out_shape=jax.ShapeDtypeStruct((slots, rlen, enc), BF16),
        compiler_params=pltpu.CompilerParams(vmem_limit_bytes=24 * 1024 * 1024),
        cost_estimate=pl.CostEstimate(
            flops=count * rlen * enc,
            bytes_accessed=2 * (count + slots) * rlen * enc,
            transcendentals=0,
        ),
        name="fold",
    )(slot_ids, returned)


def partial_kernel(layout, parts, here, *refs):
    ring = 4
    count = len(layout)
    a_own, a_peer = refs[:2]
    b_refs = refs[2 : 2 + 2 * count]
    outs = refs[2 + 2 * count : 2 + 2 * count + 4 * len(parts)]
    power_ref = refs[2 + 2 * count + 4 * len(parts)]
    totals = refs[3 + 2 * count + 4 * len(parts) :]
    lanes = outs[0].shape[1]
    powers = []
    for i, total in enumerate(totals):
        total[...] = tn(a_own[...], b_refs[2 * i][...]) + tn(a_peer[...], b_refs[2 * i + 1][...])
        top = jnp.max(jnp.abs(total[...]).reshape(-1, 8, total.shape[1]), axis=0)
        top = jnp.full((8, 128), jnp.max(top))
        powers.append(jnp.clip(jnp.floor(jnp.log2(top)), -100.0, 127.0))
    for i in range(2):
        power = powers[min(i, count - 1)]
        head = power * jnp.exp2(power - 14.0)
        for n in range(lanes // 128):
            at = slice(n * 128, (n + 1) * 128)
            power_ref[8 * i : 8 * i + 8, at] = power
            for out in outs:
                size = out.shape[0] - 16
                out[size + 8 * i : size + 8 * i + 8, at] = head

    def fill(out, by, first, end):
        pieces = []
        for total, (slices, rows, _) in zip(totals, layout):
            chunk = total.shape[0] // ring
            at = pl.multiple_of(lax.rem(here[0] + by, ring) * chunk, 8)
            for n in range(slices):
                pieces.append((total[pl.ds(at, chunk), n * lanes : (n + 1) * lanes], rows))
        at = 0
        if len(pieces) == 1:
            piece, rows = pieces[0]
            out[0 : (end - first) * rows, :] = piece[first * rows : end * rows]
            return
        for dest in range(first, end):
            for piece, rows in pieces:
                out[at : at + rows, :] = piece[dest * rows : (dest + 1) * rows]
                at += rows
                fill_up = -rows % 8
                if fill_up:
                    out[at : at + fill_up, :] = jnp.zeros((fill_up, lanes), F32)
                at += fill_up

    for n, (first, end, near_by, wait_by) in enumerate(parts):
        for out, by in zip(outs[4 * n : 4 * n + 4], (2, near_by, wait_by, 0)):
            fill(out, by, first, end)


def partial(here, lanes, a_own, a_peer, pairs, parts):
    count = lax.axis_size("seq")
    ring = lax.axis_size("dp")
    assert ring == 4
    toks, rows = a_own.shape
    per = rows // (ring * count)
    layout = [(b.shape[1] // lanes, per, -per % 8) for b, _ in pairs]
    size = sum(n * (r + fill) for n, r, fill in layout)
    operands = [a_own, a_peer] + [b for pair in pairs for b in pair]

    def whole(shape):
        return pl.BlockSpec(shape, lambda i, h: (0, 0))

    shapes = []
    for first, end, _, _ in parts:
        shapes += [((end - first) * size + 16, lanes)] * 4
    shapes.append((16, lanes))
    cols = sum(b.shape[1] for b, _ in pairs)
    outs = pl.pallas_call(
        functools.partial(partial_kernel, layout, parts),
        grid_spec=pltpu.PrefetchScalarGridSpec(
            num_scalar_prefetch=1,
            grid=(1,),
            in_specs=[whole(x.shape) for x in operands],
            out_specs=[whole(shape) for shape in shapes],
            scratch_shapes=[pltpu.VMEM((rows, b.shape[1]), F32) for b, _ in pairs],
        ),
        out_shape=[jax.ShapeDtypeStruct(shape, F32) for shape in shapes],
        compiler_params=pltpu.CompilerParams(vmem_limit_bytes=40 * 1024 * 1024),
        cost_estimate=pl.CostEstimate(
            flops=8 * toks * rows * cols,
            bytes_accessed=4 * toks * (rows + cols) + 4 * rows * cols,
            transcendentals=0,
        ),
        name="partial",
    )(here, *operands)
    powers = (outs[-1][0:1], outs[-1][8:9])
    return [outs[4 * n : 4 * n + 4] for n in range(len(parts))], powers


def by_row(shape, first, second):
    rows = lax.broadcasted_iota(jnp.int32, shape, 0)
    return jnp.where(lax.rem(rows, 16) < 8, first, second)


def up(shape, powers):
    return by_row(shape, *(jnp.exp2(14.0 - p) for p in powers))


def down(shape, powers):
    return by_row(shape, *(jnp.exp2(p - 14.0) for p in powers))


def above(*powers):
    tops = [functools.reduce(jnp.maximum, p) for p in zip(*powers)]
    return [jnp.clip(t + float(len(powers) - 1), -100.0, 127.0) for t in tops]


def moved(x, way):
    return lax.ppermute(x, "dp", [(i, (i + way) % 4) for i in range(4)])


def heads(x):
    return x[-16:-15].astype(F32), x[-8:-7].astype(F32)


def ring_start(part, powers):
    far, near = part[:2]
    return [(x * up(x.shape, powers)).astype(HALF) for x in (far, near)]


def ring_middle(part, powers, far):
    shape = far.shape
    theirs = heads(far)
    tops = above(powers, theirs)
    both = (part[2] + far.astype(F32) * down(shape, theirs)) * up(shape, tops)
    is_head = lax.broadcasted_iota(jnp.int32, shape, 0) >= shape[0] - 16
    return jnp.where(is_head, by_row(shape, *tops), both).astype(HALF)


def ring_end(part, powers, near, two):
    shape = near.shape
    near_powers, two_powers = heads(near), heads(two)
    total = (
        part[3]
        + near.astype(F32) * down(shape, near_powers)
        + two.astype(F32) * down(shape, two_powers)
    )
    return total, above(powers, near_powers, two_powers)


def for_seq(q, o, kv_low, kv_high):
    count = lax.axis_size("seq")
    lanes = q[0].shape[1]
    quarter = lanes // 4
    tops = [jnp.maximum(a, b) for a, b in zip(kv_low[1], kv_high[1])]
    powers = (q[1][0], o[1][0], tops[0], tops[1])

    def halves(x, tops):
        x = x[0][: x[0].shape[0] - 16]
        return (x * up(x.shape, tops)).astype(HALF)

    def with_powers(x):
        rows = lax.broadcasted_iota(jnp.int32, x.shape, 0)
        lane = lax.broadcasted_iota(jnp.int32, (1, lanes), 1) // quarter
        mark = jnp.where(
            lane < 2,
            jnp.where(lane == 0, powers[0], powers[1]),
            jnp.where(lane == 2, powers[2], powers[3]),
        )
        return jnp.where(lax.rem(rows, 16) == 7, mark.astype(HALF), x)

    blocks = (
        halves(q, q[1]),
        halves(o, o[1]),
        with_powers(halves(kv_low, tops)),
        with_powers(halves(kv_high, tops)),
    )
    q, o, kv_low, kv_high = lax.optimization_barrier(blocks)
    kv = jnp.concatenate([kv_low, kv_high], axis=0)
    q, o, kv = (x.reshape(count, -1, lanes) for x in (q, o, kv))
    return jnp.concatenate([q, o, kv], axis=1), q.shape[1], o.shape[1]


def finish_kernel(rows, x_ref, *outs):
    count, _, lanes = x_ref.shape
    quarter = lanes // 4
    mark = sum(slices * n for slices, n in rows[:2]) + 7
    for side in range(2):
        totals = [None] * 4
        for sender in range(side, count, 2):
            scale = jnp.exp2(x_ref[sender, mark : mark + 1, :] - 14.0)
            at = 0
            for i, (slices, n) in enumerate(rows):
                size = slices * (n + -n % 8)
                one = jnp.concatenate([scale[:, i * quarter : (i + 1) * quarter]] * 4, axis=1)
                block = x_ref[sender, at : at + size, :] * one
                totals[i] = block if totals[i] is None else totals[i] + block
                at += size
        for (slices, n), total, out in zip(rows, totals, outs):
            for j in range(slices):
                to = (side * slices + j) * lanes
                out[:, to : to + lanes] = total[j * n : (j + 1) * n]


def summed_over_seq(sent, n_q, n_o):
    _, _, lanes = sent.shape
    got = lax.all_to_all(sent, "seq", split_axis=0, concat_axis=0, tiled=True)
    n_o //= 2
    rows = [(1, n_q), (2, n_o), (1, 7), (1, 7)]
    out = [jax.ShapeDtypeStruct((n, 2 * slices * lanes), F32) for slices, n in rows]
    return pl.pallas_call(
        functools.partial(finish_kernel, rows),
        out_shape=out,
        compiler_params=pltpu.CompilerParams(vmem_limit_bytes=24 * 1024 * 1024),
        cost_estimate=pl.CostEstimate(
            flops=2 * got.size, bytes_accessed=4 * got.size, transcendentals=0
        ),
        name="finish",
    )(got.astype(F32))


def local(
    hidden,
    grad_out,
    nbr_owner,
    send_slots,
    encodings,
    weight_query,
    weight_key,
    weight_value,
    weight_out,
):
    rim = GROUP - 1
    tok_rows = hidden[0]
    cot_rows = grad_out[0]
    toks, width = tok_rows.shape
    own = encodings[0]
    slots, rlen, enc = own.shape
    count = lax.axis_size("seq")
    core = lax.rem(lax.axis_index("seq"), 2)
    is_first = core == 0

    heads = jnp.concatenate([tok_rows[:rim], cot_rows[:rim]], axis=1)
    heads = passed_along(heads, "seq", -1)

    slot_ids = send_slots[0, 0].reshape(-1)
    outgoing = own.at[slot_ids].get(mode="promise_in_bounds")
    outgoing, heads = lax.optimization_barrier((outgoing, heads))
    incoming = lax.all_to_all(outgoing, "seq", split_axis=0, concat_axis=0, tiled=True)
    pos = nbr_owner[0].reshape(-1)

    query_rows = jnp.concatenate([tok_rows[rim:], heads[:, :width]], axis=0)
    grad_rows = jnp.concatenate([cot_rows[rim:], heads[:, width:]], axis=0)
    queries = nn(query_rows, weight_query).astype(BF16)
    d_context = nt(grad_rows, weight_out).astype(BF16)
    left, right = grad_rows[:, : width // 2], grad_rows[:, width // 2 :]
    grad_mine = jnp.where(is_first, left, right)
    query_peer, grad_peer = swapped((query_rows, jnp.where(is_first, right, left)))
    queries, d_context, grad_mine = lax.optimization_barrier((queries, d_context, grad_mine))
    owner_ids = lax.broadcasted_iota(jnp.int32, (count, pos.shape[0]), 0)
    named = jnp.sum((owner_ids == pos[None, :]).astype(jnp.int32), axis=1)

    (
        context,
        d_queries,
        dq_mine,
        dq_other,
        dk_mine,
        dk_other,
        dv_mine,
        dv_other,
        rows,
        tails,
        send_back,
    ) = attend(
        pos,
        named,
        core.reshape(1),
        incoming,
        queries,
        d_context,
        weight_key,
        weight_value,
        weight_key.T,
        weight_value.T,
    )
    returned = lax.all_to_all(send_back, "seq", split_axis=0, concat_axis=0, tiled=True)

    tails = passed_along(tails, "seq", 1)

    here = lax.axis_index("dp").reshape(1)
    half = dq_mine.shape[1]
    dq_peer, context_peer = swapped((dq_other, context))
    dk_peer, dv_peer, rows_peer = swapped((dk_other, dv_other, rows))
    (part_q,), power_q = partial(
        here, half, query_rows, query_peer, [(dq_mine, dq_peer)], [(0, count, 3, 1)]
    )
    first_q = ring_start(part_q, power_q)
    first_q, context_peer = lax.optimization_barrier((first_q, context_peer))
    far_q, near_q = moved(first_q[0], 1), moved(first_q[1], -1)
    (part_o,), power_o = partial(
        here, half, context, context_peer, [(grad_mine, grad_peer)], [(0, count, 1, 3)]
    )
    first_o = ring_start(part_o, power_o)
    kv_inputs = (rows, rows_peer, dk_mine, dk_peer, dv_mine, dv_peer)
    first_o, kv_inputs = lax.optimization_barrier((first_o, kv_inputs))
    far_o, near_o = moved(first_o[0], -1), moved(first_o[1], 1)
    (part_low, part_high), power_kv = partial(
        here,
        half,
        kv_inputs[0],
        kv_inputs[1],
        [kv_inputs[2:4], kv_inputs[4:6]],
        [(0, count // 2, 3, 1), (count // 2, count, 1, 3)],
    )
    second = [ring_start(part_low, power_kv), ring_start(part_high, power_kv)]
    far_q, far_o, second = lax.optimization_barrier((far_q, far_o, second))
    far_low, near_low = moved(second[0][0], 1), moved(second[0][1], -1)
    far_high, near_high = moved(second[1][0], -1), moved(second[1][1], 1)
    two_q = ring_middle(part_q, power_q, far_q)
    two_o = ring_middle(part_o, power_o, far_o)
    two_q, two_o, far_low, far_high = lax.optimization_barrier((two_q, two_o, far_low, far_high))
    two_q, two_o = moved(two_q, 1), moved(two_o, -1)
    two_low = moved(ring_middle(part_low, power_kv, far_low), 1)
    two_high = moved(ring_middle(part_high, power_kv, far_high), -1)
    sum_q = ring_end(part_q, power_q, near_q, two_q)
    sum_o = ring_end(part_o, power_o, near_o, two_o)
    sum_low = ring_end(part_low, power_kv, near_low, two_low)
    sum_high = ring_end(part_high, power_kv, near_high, two_high)
    sent, n_q, n_o = for_seq(sum_q, sum_o, sum_low, sum_high)
    returned, sent, tails = lax.optimization_barrier((returned, sent, tails))
    share_q, share_o, share_k, share_v = summed_over_seq(sent, n_q, n_o)

    inner = context.shape[1]
    context = jnp.concatenate([tails[1:, :inner], context[: toks - rim]], axis=0)
    d_queries = jnp.concatenate([tails[1:, inner:], d_queries[: toks - rim]], axis=0)
    mixed = nn(context, weight_out).astype(BF16)[None]
    grad_hidden = nt(d_queries, weight_query).astype(BF16)[None]
    grad_own = fold(slot_ids, returned, slots)[None]
    return (mixed, grad_hidden, grad_own, share_q, share_k, share_v, share_o)


def solution(mesh):
    return jax.shard_map(
        local,
        mesh=mesh,
        in_specs=(
            P("dp", "seq", None),
            P("dp", "seq", None),
            P("dp", "seq", None),
            P("dp", "seq", None, None),
            P("dp", "seq", None, None),
            P(),
            P(),
            P(),
            P(),
        ),
        out_specs=(
            P("dp", "seq", None),
            P("dp", "seq", None),
            P("dp", "seq", None, None),
            P(("dp", "seq"), None),
            P(("dp", "seq"), None),
            P(("dp", "seq"), None),
            P(("dp", "seq"), None),
        ),
        check_vma=False,
    )
```

```python
import functools

import jax
import jax.numpy as jnp
from jax import lax
from jax.experimental import pallas as pl
from jax.experimental.pallas import tpu as pltpu
from jax.sharding import PartitionSpec as P

HEADS = 8
GROUP = 64
NBR = 2

F32 = jnp.float32
BF16 = jnp.bfloat16
HALF = jnp.float16
VMEM = 56 * 1024 * 1024


def nn(a, b):
    return lax.dot_general(a, b, (((1,), (0,)), ((), ())), preferred_element_type=F32)


def nt(a, b):
    return lax.dot_general(a, b, (((1,), (1,)), ((), ())), preferred_element_type=F32)


def tn(a, b):
    return lax.dot_general(a, b, (((0,), (0,)), ((), ())), preferred_element_type=F32)


def passed_along(x, axis, by):
    count = lax.axis_size(axis)
    pairs = [(i, i + by) for i in range(count) if 0 <= i + by < count]
    return lax.ppermute(x, axis, pairs)


def swapped(x):
    count = lax.axis_size("seq")
    return lax.ppermute(x, "seq", [(i, i ^ 1) for i in range(count)])


def attend_kernel(
    pos,
    named,
    core,
    enc_a,
    enc_b,
    q_ref,
    dc_ref,
    wk,
    wv,
    wkt,
    wvt,
    ctx_ref,
    dq_ref,
    dq_mine,
    dq_other,
    dk_mine,
    dk_other,
    dv_mine,
    dv_other,
    rows_ref,
    tail_ref,
    back_ref,
    k_all,
    v_all,
    dk_all,
    dv_all,
    d_rows,
    blank,
    sent,
    blanked,
):
    rlen = enc_a.shape[1]
    inner = q_ref.shape[1]
    size = inner // HEADS
    half_heads = HEADS // 2
    scale = size**-0.5
    step = pl.program_id(0)
    last = pl.num_programs(0) - 1

    def blanking(act):
        for owner in range(back_ref.shape[0]):

            @pl.when(named[owner] == 0)
            def _():
                act(pltpu.make_async_copy(blank, back_ref.at[owner], blanked))

    @pl.when(step == 0)
    def _():
        blank[...] = jnp.zeros_like(blank)
        blanking(lambda copy: copy.start())

    rows_ref[0:rlen, :] = enc_a[0]
    rows_ref[rlen : 2 * rlen, :] = enc_b[0]
    rows = rows_ref[...]
    k_all[...] = nn(rows, wk[...]).astype(BF16)
    v_all[...] = nn(rows, wv[...]).astype(BF16)
    units = []
    for side, halves in enumerate(
        ((dq_mine, dk_mine, dv_mine), (dq_other, dk_other, dv_other))
    ):
        half = core[0] if side == 0 else 1 - core[0]
        for h in range(half_heads):
            cols = pl.ds(pl.multiple_of(half * (inner // 2) + h * size, size), size)
            units.append((cols, slice(h * size, (h + 1) * size)) + halves)
    scores = [nt(q_ref[:, u[0]], k_all[:, u[0]]) * scale for u in units]
    d_probs = [nt(dc_ref[:, u[0]], v_all[:, u[0]]) for u in units]
    lifted = [jnp.exp(s - jnp.max(s, axis=-1, keepdims=True)) for s in scores]
    probs = [x * (1.0 / jnp.sum(x, axis=-1, keepdims=True)) for x in lifted]
    probs_b = [p.astype(BF16) for p in probs]
    for (cols, here, _, _, dv_half), p in zip(units, probs_b):
        ctx_ref[:, cols] = nn(p, v_all[:, cols]).astype(BF16)
    for (cols, here, _, _, dv_half), p in zip(units, probs_b):
        dv = tn(p, dc_ref[:, cols]).astype(BF16)
        dv_all[:, cols] = dv
        dv_half[:, here] = dv
    d_scores = [
        (scale * p * (d - jnp.sum(p * d, axis=-1, keepdims=True))).astype(BF16)
        for p, d in zip(probs, d_probs)
    ]
    for (cols, here, dq_half, _, _), d in zip(units, d_scores):
        dq = nn(d, k_all[:, cols]).astype(BF16)
        dq_ref[:, cols] = dq
        dq_half[:, here] = dq
    for (cols, here, _, dk_half, _), d in zip(units, d_scores):
        dk = tn(d, q_ref[:, cols]).astype(BF16)
        dk_all[:, cols] = dk
        dk_half[:, here] = dk

    def sending(at):
        return [
            pltpu.make_async_copy(d_rows.at[n], back_ref.at[pos[NBR * at + n]], sent.at[n])
            for n in range(NBR)
        ]

    @pl.when(step > 0)
    def _():
        for copy in sending(step - 1):
            copy.wait()

    for n in range(NBR):
        mine = slice(n * rlen, (n + 1) * rlen)
        total = nn(dk_all[mine, :], wkt[...]) + nn(dv_all[mine, :], wvt[...])
        d_rows[n] = total.astype(BF16)
    for copy in sending(step):
        copy.start()

    @pl.when(step == last)
    def _():
        tail_ref[:, :inner] = ctx_ref[...]
        tail_ref[:, inner:] = dq_ref[...]
        for copy in sending(step):
            copy.wait()
        blanking(lambda copy: copy.wait())


def attend(pos, named, core, incoming, projected, wk, wv, wkt, wvt):
    owners, rlen, enc = incoming.shape
    toks, inner = projected.shape[0], projected.shape[1] // 2
    groups = toks // GROUP
    keys = NBR * rlen
    half = inner // 2

    def whole(x):
        return pl.BlockSpec(x.shape, lambda c, *_: (0, 0))

    def by_group(rows, cols):
        return pl.BlockSpec((rows, cols), lambda c, *_: (c, 0))

    grid_spec = pltpu.PrefetchScalarGridSpec(
        num_scalar_prefetch=3,
        grid=(groups,),
        in_specs=[
            pl.BlockSpec((1, rlen, enc), lambda c, pos, named, core: (pos[NBR * c], 0, 0)),
            pl.BlockSpec((1, rlen, enc), lambda c, pos, named, core: (pos[NBR * c + 1], 0, 0)),
            by_group(GROUP, inner),
            pl.BlockSpec((GROUP, inner), lambda c, *_: (c, 1)),
            whole(wk),
            whole(wv),
            whole(wkt),
            whole(wvt),
        ],
        out_specs=[
            by_group(GROUP, inner),
            by_group(GROUP, inner),
            by_group(GROUP, half),
            by_group(GROUP, half),
            by_group(keys, half),
            by_group(keys, half),
            by_group(keys, half),
            by_group(keys, half),
            by_group(keys, enc),
            pl.BlockSpec((GROUP, 2 * inner), lambda c, *_: (0, 0)),
            pl.BlockSpec(memory_space=pl.ANY),
        ],
        scratch_shapes=[pltpu.VMEM((keys, inner), BF16)] * 4
        + [
            pltpu.VMEM((NBR, rlen, enc), BF16),
            pltpu.VMEM((rlen, enc), BF16),
            pltpu.SemaphoreType.DMA((NBR,)),
            pltpu.SemaphoreType.DMA,
        ],
    )
    tok = jax.ShapeDtypeStruct((toks, inner), BF16)
    tok_half = jax.ShapeDtypeStruct((toks, half), BF16)
    key_half = jax.ShapeDtypeStruct((groups * keys, half), BF16)
    flops = 2 * groups * keys * enc * inner * 4 + 14 * toks * keys * inner
    return pl.pallas_call(
        attend_kernel,
        grid_spec=grid_spec,
        out_shape=[
            tok,
            tok,
            tok_half,
            tok_half,
            key_half,
            key_half,
            key_half,
            key_half,
            jax.ShapeDtypeStruct((groups * keys, enc), BF16),
            jax.ShapeDtypeStruct((GROUP, 2 * inner), BF16),
            jax.ShapeDtypeStruct(incoming.shape, BF16),
        ],
        compiler_params=pltpu.CompilerParams(vmem_limit_bytes=VMEM),
        cost_estimate=pl.CostEstimate(
            flops=flops, bytes_accessed=40_000_000, transcendentals=toks * keys * HEADS
        ),
        name="attend",
    )(pos, named, core, incoming, incoming, projected, projected, wk, wv, wkt, wvt)


def fold_kernel(slot_ids, x_ref, out_ref, total):
    total[...] = jnp.zeros_like(total)
    for i in range(x_ref.shape[0]):
        total[slot_ids[i]] += x_ref[i].astype(F32)
    out_ref[...] = total[...].astype(BF16)


def fold(slot_ids, returned, slots):
    count, rlen, enc = returned.shape
    rows = 16
    return pl.pallas_call(
        fold_kernel,
        grid_spec=pltpu.PrefetchScalarGridSpec(
            num_scalar_prefetch=1,
            grid=(rlen // rows,),
            in_specs=[pl.BlockSpec((count, rows, enc), lambda i, s: (0, i, 0))],
            out_specs=pl.BlockSpec((slots, rows, enc), lambda i, s: (0, i, 0)),
            scratch_shapes=[pltpu.VMEM((slots, rows, enc), F32)],
        ),
        out_shape=jax.ShapeDtypeStruct((slots, rlen, enc), BF16),
        compiler_params=pltpu.CompilerParams(vmem_limit_bytes=24 * 1024 * 1024),
        cost_estimate=pl.CostEstimate(
            flops=count * rlen * enc,
            bytes_accessed=2 * (count + slots) * rlen * enc,
            transcendentals=0,
        ),
        name="fold",
    )(slot_ids, returned)


def partial_kernel(layout, parts, here, *refs):
    ring = 4
    count = len(layout)
    a_own, a_peer = refs[:2]
    b_refs = refs[2 : 2 + 2 * count]
    outs = refs[2 + 2 * count : 2 + 2 * count + 4 * len(parts)]
    power_ref = refs[2 + 2 * count + 4 * len(parts)]
    totals = refs[3 + 2 * count + 4 * len(parts) :]
    lanes = outs[0].shape[1]
    powers = []
    for i, total in enumerate(totals):
        total[...] = tn(a_own[...], b_refs[2 * i][...]) + tn(a_peer[...], b_refs[2 * i + 1][...])
        top = jnp.max(jnp.abs(total[...]).reshape(-1, 8, total.shape[1]), axis=0)
        top = jnp.full((8, 128), jnp.max(top))
        powers.append(jnp.clip(jnp.floor(jnp.log2(top)), -100.0, 127.0))
    for i in range(2):
        power = powers[min(i, count - 1)]
        head = power * jnp.exp2(power - 14.0)
        for n in range(lanes // 128):
            at = slice(n * 128, (n + 1) * 128)
            power_ref[8 * i : 8 * i + 8, at] = power
            for out in outs:
                size = out.shape[0] - 16
                out[size + 8 * i : size + 8 * i + 8, at] = head

    def fill(out, by, first, end):
        pieces = []
        for total, (slices, rows, _) in zip(totals, layout):
            chunk = total.shape[0] // ring
            at = pl.multiple_of(lax.rem(here[0] + by, ring) * chunk, 8)
            for n in range(slices):
                pieces.append((total[pl.ds(at, chunk), n * lanes : (n + 1) * lanes], rows))
        at = 0
        if len(pieces) == 1:
            piece, rows = pieces[0]
            out[0 : (end - first) * rows, :] = piece[first * rows : end * rows]
            return
        for dest in range(first, end):
            for piece, rows in pieces:
                out[at : at + rows, :] = piece[dest * rows : (dest + 1) * rows]
                at += rows
                fill_up = -rows % 8
                if fill_up:
                    out[at : at + fill_up, :] = jnp.zeros((fill_up, lanes), F32)
                at += fill_up

    for n, (first, end, near_by, wait_by) in enumerate(parts):
        for out, by in zip(outs[4 * n : 4 * n + 4], (2, near_by, wait_by, 0)):
            fill(out, by, first, end)


def partial(here, lanes, a_own, a_peer, pairs, parts):
    count = lax.axis_size("seq")
    ring = lax.axis_size("dp")
    assert ring == 4
    toks, rows = a_own.shape
    per = rows // (ring * count)
    layout = [(b.shape[1] // lanes, per, -per % 8) for b, _ in pairs]
    size = sum(n * (r + fill) for n, r, fill in layout)
    operands = [a_own, a_peer] + [b for pair in pairs for b in pair]

    def whole(shape):
        return pl.BlockSpec(shape, lambda i, h: (0, 0))

    shapes = []
    for first, end, _, _ in parts:
        shapes += [((end - first) * size + 16, lanes)] * 4
    shapes.append((16, lanes))
    cols = sum(b.shape[1] for b, _ in pairs)
    outs = pl.pallas_call(
        functools.partial(partial_kernel, layout, parts),
        grid_spec=pltpu.PrefetchScalarGridSpec(
            num_scalar_prefetch=1,
            grid=(1,),
            in_specs=[whole(x.shape) for x in operands],
            out_specs=[whole(shape) for shape in shapes],
            scratch_shapes=[pltpu.VMEM((rows, b.shape[1]), F32) for b, _ in pairs],
        ),
        out_shape=[jax.ShapeDtypeStruct(shape, F32) for shape in shapes],
        compiler_params=pltpu.CompilerParams(vmem_limit_bytes=40 * 1024 * 1024),
        cost_estimate=pl.CostEstimate(
            flops=8 * toks * rows * cols,
            bytes_accessed=4 * toks * (rows + cols) + 4 * rows * cols,
            transcendentals=0,
        ),
        name="partial",
    )(here, *operands)
    powers = (outs[-1][0:1], outs[-1][8:9])
    return [outs[4 * n : 4 * n + 4] for n in range(len(parts))], powers


def by_row(shape, first, second):
    rows = lax.broadcasted_iota(jnp.int32, shape, 0)
    return jnp.where(lax.rem(rows, 16) < 8, first, second)


def up(shape, powers):
    return by_row(shape, *(jnp.exp2(14.0 - p) for p in powers))


def down(shape, powers):
    return by_row(shape, *(jnp.exp2(p - 14.0) for p in powers))


def above(*powers):
    tops = [functools.reduce(jnp.maximum, p) for p in zip(*powers)]
    return [jnp.clip(t + float(len(powers) - 1), -100.0, 127.0) for t in tops]


def moved(x, way):
    return lax.ppermute(x, "dp", [(i, (i + way) % 4) for i in range(4)])


def heads(x):
    return x[-16:-15].astype(F32), x[-8:-7].astype(F32)


def ring_start(part, powers):
    far, near = part[:2]
    return [(x * up(x.shape, powers)).astype(HALF) for x in (far, near)]


def ring_middle(part, powers, far):
    shape = far.shape
    theirs = heads(far)
    tops = above(powers, theirs)
    both = (part[2] + far.astype(F32) * down(shape, theirs)) * up(shape, tops)
    is_head = lax.broadcasted_iota(jnp.int32, shape, 0) >= shape[0] - 16
    return jnp.where(is_head, by_row(shape, *tops), both).astype(HALF)


def ring_end(part, powers, near, two):
    shape = near.shape
    near_powers, two_powers = heads(near), heads(two)
    total = (
        part[3]
        + near.astype(F32) * down(shape, near_powers)
        + two.astype(F32) * down(shape, two_powers)
    )
    return total, above(powers, near_powers, two_powers)


def for_seq(q, o, kv_low, kv_high):
    count = lax.axis_size("seq")
    lanes = q[0].shape[1]
    quarter = lanes // 4
    tops = [jnp.maximum(a, b) for a, b in zip(kv_low[1], kv_high[1])]
    powers = (q[1][0], o[1][0], tops[0], tops[1])

    def halves(x, tops):
        x = x[0][: x[0].shape[0] - 16]
        return (x * up(x.shape, tops)).astype(HALF)

    def with_powers(x):
        rows = lax.broadcasted_iota(jnp.int32, x.shape, 0)
        lane = lax.broadcasted_iota(jnp.int32, (1, lanes), 1) // quarter
        mark = jnp.where(
            lane < 2,
            jnp.where(lane == 0, powers[0], powers[1]),
            jnp.where(lane == 2, powers[2], powers[3]),
        )
        return jnp.where(lax.rem(rows, 16) == 7, mark.astype(HALF), x)

    blocks = (
        halves(q, q[1]),
        halves(o, o[1]),
        with_powers(halves(kv_low, tops)),
        with_powers(halves(kv_high, tops)),
    )
    q, o, kv_low, kv_high = lax.optimization_barrier(blocks)
    kv = jnp.concatenate([kv_low, kv_high], axis=0)
    q, o, kv = (x.reshape(count, -1, lanes) for x in (q, o, kv))
    return jnp.concatenate([q, o, kv], axis=1), q.shape[1], o.shape[1]


def finish_kernel(rows, x_ref, *outs):
    count, _, lanes = x_ref.shape
    quarter = lanes // 4
    mark = sum(slices * n for slices, n in rows[:2]) + 7
    for side in range(2):
        totals = [None] * 4
        for sender in range(side, count, 2):
            scale = jnp.exp2(x_ref[sender, mark : mark + 1, :] - 14.0)
            at = 0
            for i, (slices, n) in enumerate(rows):
                size = slices * (n + -n % 8)
                one = jnp.concatenate([scale[:, i * quarter : (i + 1) * quarter]] * 4, axis=1)
                block = x_ref[sender, at : at + size, :] * one
                totals[i] = block if totals[i] is None else totals[i] + block
                at += size
        for (slices, n), total, out in zip(rows, totals, outs):
            for j in range(slices):
                to = (side * slices + j) * lanes
                out[:, to : to + lanes] = total[j * n : (j + 1) * n]


def summed_over_seq(sent, n_q, n_o):
    _, _, lanes = sent.shape
    got = lax.all_to_all(sent, "seq", split_axis=0, concat_axis=0, tiled=True)
    n_o //= 2
    rows = [(1, n_q), (2, n_o), (1, 7), (1, 7)]
    out = [jax.ShapeDtypeStruct((n, 2 * slices * lanes), F32) for slices, n in rows]
    return pl.pallas_call(
        functools.partial(finish_kernel, rows),
        out_shape=out,
        compiler_params=pltpu.CompilerParams(vmem_limit_bytes=24 * 1024 * 1024),
        cost_estimate=pl.CostEstimate(
            flops=2 * got.size, bytes_accessed=4 * got.size, transcendentals=0
        ),
        name="finish",
    )(got.astype(F32))


def local(
    hidden,
    grad_out,
    nbr_owner,
    send_slots,
    encodings,
    weight_query,
    weight_key,
    weight_value,
    weight_out,
):
    rim = GROUP - 1
    tok_rows = hidden[0]
    cot_rows = grad_out[0]
    toks, width = tok_rows.shape
    own = encodings[0]
    slots, rlen, enc = own.shape
    count = lax.axis_size("seq")
    core = lax.rem(lax.axis_index("seq"), 2)
    is_first = core == 0

    heads = jnp.concatenate([tok_rows[:rim], cot_rows[:rim]], axis=1)
    heads = passed_along(heads, "seq", -1)

    slot_ids = send_slots[0, 0].reshape(-1)
    outgoing = own.at[slot_ids].get(mode="promise_in_bounds")
    incoming = lax.all_to_all(outgoing, "seq", split_axis=0, concat_axis=0, tiled=True)
    pos = nbr_owner[0].reshape(-1)

    projected = jnp.concatenate(
        [nn(tok_rows, weight_query).astype(BF16), nt(cot_rows, weight_out).astype(BF16)], axis=1
    )
    next_rows = passed_along(projected[:rim], "seq", -1)
    projected = jnp.pad(projected[rim:], ((0, rim), (0, 0)))
    projected, incoming, next_rows = lax.optimization_barrier((projected, incoming, next_rows))
    projected = lax.dynamic_update_slice(projected, next_rows, (toks - rim, 0))
    owner_ids = lax.broadcasted_iota(jnp.int32, (count, pos.shape[0]), 0)
    named = jnp.sum((owner_ids == pos[None, :]).astype(jnp.int32), axis=1)

    (
        context,
        d_queries,
        dq_mine,
        dq_other,
        dk_mine,
        dk_other,
        dv_mine,
        dv_other,
        rows,
        tails,
        send_back,
    ) = attend(
        pos,
        named,
        core.reshape(1),
        incoming,
        projected,
        weight_key,
        weight_value,
        weight_key.T,
        weight_value.T,
    )
    returned = lax.all_to_all(send_back, "seq", split_axis=0, concat_axis=0, tiled=True)

    heads, tails = lax.optimization_barrier((heads, tails))
    query_rows = jnp.concatenate([tok_rows[rim:], heads[:, :width]], axis=0)
    grad_rows = jnp.concatenate([cot_rows[rim:], heads[:, width:]], axis=0)
    left, right = grad_rows[:, : width // 2], grad_rows[:, width // 2 :]
    grad_mine = jnp.where(is_first, left, right)
    query_peer, grad_peer = swapped((query_rows, jnp.where(is_first, right, left)))
    tails = passed_along(tails, "seq", 1)

    here = lax.axis_index("dp").reshape(1)
    half = dq_mine.shape[1]
    dq_peer, context_peer = swapped((dq_other, context))
    dk_peer, dv_peer, rows_peer = swapped((dk_other, dv_other, rows))
    (part_q,), power_q = partial(
        here, half, query_rows, query_peer, [(dq_mine, dq_peer)], [(0, count, 3, 1)]
    )
    first_q = ring_start(part_q, power_q)
    first_q, context_peer = lax.optimization_barrier((first_q, context_peer))
    far_q, near_q = moved(first_q[0], 1), moved(first_q[1], -1)
    (part_o,), power_o = partial(
        here, half, context, context_peer, [(grad_mine, grad_peer)], [(0, count, 1, 3)]
    )
    first_o = ring_start(part_o, power_o)
    kv_inputs = (rows, rows_peer, dk_mine, dk_peer, dv_mine, dv_peer)
    first_o, kv_inputs = lax.optimization_barrier((first_o, kv_inputs))
    far_o, near_o = moved(first_o[0], -1), moved(first_o[1], 1)
    (part_low, part_high), power_kv = partial(
        here,
        half,
        kv_inputs[0],
        kv_inputs[1],
        [kv_inputs[2:4], kv_inputs[4:6]],
        [(0, count // 2, 3, 1), (count // 2, count, 1, 3)],
    )
    second = [ring_start(part_low, power_kv), ring_start(part_high, power_kv)]
    far_q, far_o, second = lax.optimization_barrier((far_q, far_o, second))
    far_low, near_low = moved(second[0][0], 1), moved(second[0][1], -1)
    far_high, near_high = moved(second[1][0], -1), moved(second[1][1], 1)
    two_q = ring_middle(part_q, power_q, far_q)
    two_o = ring_middle(part_o, power_o, far_o)
    two_q, two_o, far_low, far_high = lax.optimization_barrier((two_q, two_o, far_low, far_high))
    two_q, two_o = moved(two_q, 1), moved(two_o, -1)
    two_low = moved(ring_middle(part_low, power_kv, far_low), 1)
    two_high = moved(ring_middle(part_high, power_kv, far_high), -1)
    sum_q = ring_end(part_q, power_q, near_q, two_q)
    sum_o = ring_end(part_o, power_o, near_o, two_o)
    sum_low = ring_end(part_low, power_kv, near_low, two_low)
    sum_high = ring_end(part_high, power_kv, near_high, two_high)
    sent, n_q, n_o = for_seq(sum_q, sum_o, sum_low, sum_high)
    returned, sent, tails = lax.optimization_barrier((returned, sent, tails))
    share_q, share_o, share_k, share_v = summed_over_seq(sent, n_q, n_o)

    inner = context.shape[1]
    context = jnp.concatenate([tails[1:, :inner], context[: toks - rim]], axis=0)
    d_queries = jnp.concatenate([tails[1:, inner:], d_queries[: toks - rim]], axis=0)
    mixed = nn(context, weight_out).astype(BF16)[None]
    grad_hidden = nt(d_queries, weight_query).astype(BF16)[None]
    grad_own = fold(slot_ids, returned, slots)[None]
    return (mixed, grad_hidden, grad_own, share_q, share_k, share_v, share_o)


def solution(mesh):
    return jax.shard_map(
        local,
        mesh=mesh,
        in_specs=(
            P("dp", "seq", None),
            P("dp", "seq", None),
            P("dp", "seq", None),
            P("dp", "seq", None, None),
            P("dp", "seq", None, None),
            P(),
            P(),
            P(),
            P(),
        ),
        out_specs=(
            P("dp", "seq", None),
            P("dp", "seq", None),
            P("dp", "seq", None, None),
            P(("dp", "seq"), None),
            P(("dp", "seq"), None),
            P(("dp", "seq"), None),
            P(("dp", "seq"), None),
        ),
        check_vma=False,
    )
```
